256 devices in a mesh: sec: 4 (over y), ctx: 16 (over z, core), ch: 4 (over x).
Axes of the slice: x: 4, y: 4, z: 8, core: 2. Of those that a mesh axis runs over, the one named last changes fastest.
Arguments:
- inputs: bfloat16 [2048, 4096], P('ctx', ('ch', 'sec')), may hold values from -2500 to 2500, as said below
- query_fields: bfloat16 [4, 2048, 4096], P('sec', 'ctx', 'ch'), may hold values from -3 to 3
- key_fields: bfloat16 [4, 2048, 4096], P('sec', 'ctx', 'ch'), may hold values from -4 to 4
- norm_gain: float32 [4096], P('ch'), may hold values from 0.1 to 1.9
- short_taps: float32 [2, 7, 4096], P(None, None, 'ch'), may hold values from -2 to 2
- medium_taps: float32 [128, 4096], P(None, 'ch'), may hold values from -0.5 to 0.5
- pole_rates: float32 [8, 4096], P(None, 'ch'), as said below
- pole_residues: float32 [8, 4096], P(None, 'ch'), may hold values from -2 to 2
- direct_term: float32 [4096], P('ch'), may hold values from -3 to 3
Outputs:
- mixed_stream: bfloat16 [2048, 4096], P('ctx', ('ch', 'sec'))
The draws below stay inside these ranges and needn't reach their ends.
Inputs may be any that keep to these rules, and one draw needn't show every extreme that they name: `inputs`: scaled real values. `pole_rates`: Positive, from 0.2 / 2048 to 1 / 30.
All inputs are finite; a program needn't handle non-finite values.
Results may differ from the reference program's by a relative error of at most 0.013.
Values may be sent and summed in bfloat16 or wider, within the bound.
No kernel may reach another device: no remote copies, remote signals or barrier semaphores. Data moves between devices by JAX's collectives and lax.ppermute only.
A program may use at most 64 MiB of HBM per device.

```python
import math
import jax
import jax.numpy as jnp
from jax import lax

D = 4096
SHORT = 7
MEDIUM = 128
MODES = 8
SECS = 4
TOKENS = 2048
N_SEC = 4
N_CH = 4


def draw_inputs(key, part):
    rows_key, rough_key, base_key = jax.random.split(key, 3)
    rises = jnp.arange(D, dtype=jnp.float32) / D
    base_values = jax.random.truncated_normal(base_key, -6.0, 6.0, (TOKENS, D), jnp.float32)
    row_scale = jnp.exp(jax.random.uniform(rows_key, (TOKENS, 1), jnp.float32, 0.0, math.log(10.0)))
    col_scale = jnp.exp(rises * math.log(10.0))
    roughness = jax.random.uniform(rough_key, (D,), jnp.float32, 0.5, 1.5)
    return (base_values * row_scale * (col_scale * roughness)[None]).astype(jnp.bfloat16)


def draw_pole_rates(key, part):
    pick_key, slow_key, fast_key = jax.random.split(key, 3)
    grid_shape = (MODES, D)
    slow_rates = jnp.exp(jax.random.uniform(slow_key, grid_shape, jnp.float32, math.log(0.2), math.log(2.0))) / TOKENS
    fast_rates = jnp.exp(jax.random.uniform(fast_key, grid_shape, jnp.float32, math.log(2.0 / TOKENS), math.log(1.0 / 30.0)))
    slow_share = 0.5
    picked = jax.random.uniform(pick_key, grid_shape, jnp.float32) < slow_share
    return jnp.where(picked, slow_rates, fast_rates).astype(jnp.float32)


def steps_of(own_key, shape, cuts, low, high):
    gain, own = 1.0, jax.random.fold_in(own_key, 6)
    for position, blocks in cuts:
        heights = jnp.exp(jax.random.uniform(jax.random.fold_in(own, position), (blocks,), jnp.float32, low / len(cuts), high / len(cuts)))
        gain = gain * jnp.repeat(heights, shape[position] // blocks).reshape([-1 if axis == position else 1 for axis in range(len(shape))])
    return gain


def centred(own_key, shape, width, bound, cuts=(), held_as=jnp.bfloat16):
    gain = steps_of(own_key, shape, cuts, -0.22, 0.18) if cuts else 1.0
    array = jax.random.normal(own_key, shape, jnp.float32) * width * gain
    return jnp.minimum(jnp.maximum(array, -bound), bound).astype(held_as)


def setup_inputs(seed: int = 0) -> dict:
    streams_of = jax.random.split(jax.random.key(seed), 10)
    return {
        "inputs": draw_inputs(jax.random.fold_in(streams_of[9], 71), 0),
        "query_fields": centred(streams_of[1], (SECS, TOKENS, D), 0.5, 3.0, ((0, 4), (1, 16), (2, 4))),
        "key_fields": centred(streams_of[2], (SECS, TOKENS, D), 1.0, 4.0, ((0, 4), (1, 16), (2, 4))),
        "norm_gain": jnp.clip(1.0 + 0.18 * jax.random.normal(streams_of[3], (D,), jnp.float32), 0.1, 1.9),
        "short_taps": centred(streams_of[4], (2, SHORT, D), SHORT ** -0.5, 2.0, ((2, 4),), jnp.float32),
        "medium_taps": centred(streams_of[5], (MEDIUM, D), MEDIUM ** -0.5, 0.5, ((1, 4),), jnp.float32),
        "pole_rates": draw_pole_rates(jax.random.fold_in(streams_of[9], 71), 0),
        "pole_residues": centred(streams_of[7], (MODES, D), MODES ** -0.5, 2.0, ((1, 4),), jnp.float32),
        "direct_term": centred(streams_of[8], (D,), 0.5, 3.0, ((0, 4),), jnp.float32),
    }


norm_eps = 1e-06

def depthwise(padded, flipped_taps):
    channels = padded.shape[1]
    result = lax.conv_general_dilated(padded[None], flipped_taps[:, None, :], window_strides=(1,), padding='VALID', dimension_numbers=('NWC', 'WIO', 'NWC'), feature_group_count=channels, precision=lax.Precision.HIGHEST)
    return result[0]

def causal_filter(gated, filter_taps):
    span = filter_taps.shape[0]
    padded = jnp.concatenate([jnp.zeros((span - 1, gated.shape[1]), jnp.float32), gated], axis=0)
    return depthwise(padded, jnp.flip(filter_taps, 0))

def modal_recurrence(gated, rates, residues, direct):
    decays = jnp.exp(-rates)
    weights = residues * jnp.sqrt(-jnp.expm1(-2.0 * rates))

    def advance(states, new_row):
        states = decays * states + new_row[None]
        return (states, lax.optimization_barrier(jnp.sum(weights * states, axis=0)))
    initial = jnp.zeros(rates.shape, jnp.float32)
    last_state, outputs = lax.scan(advance, initial, gated)
    return outputs + direct[None] * gated

def reference(inputs, query_fields, key_fields, norm_gain, short_taps, medium_taps, pole_rates, pole_residues, direct_term):
    values = inputs.astype(jnp.float32)
    inverse_rms = lax.rsqrt(lax.optimization_barrier(jnp.mean(values * values, axis=1)) + norm_eps)
    stream = (values * inverse_rms[:, None] * norm_gain[None]).astype(jnp.bfloat16)
    block_width = D // (N_CH * N_SEC)
    block_count = N_CH * N_SEC

    def one_block(block_index):
        offset = block_index * block_width

        def channel_cut(tables):
            return lax.dynamic_slice_in_dim(tables, offset, block_width, tables.ndim - 1)
        current = channel_cut(stream)
        for section in range(4):
            query_block = channel_cut(query_fields[section])
            key_block = channel_cut(key_fields[section])
            gated = key_block.astype(jnp.float32) * current.astype(jnp.float32)
            if section == 0:
                filtered = causal_filter(gated, channel_cut(short_taps[0]))
            elif section == 1:
                filtered = causal_filter(gated, channel_cut(medium_taps))
            elif section == 2:
                filtered = modal_recurrence(gated, channel_cut(pole_rates), channel_cut(pole_residues), channel_cut(direct_term))
            else:
                filtered = causal_filter(gated, channel_cut(short_taps[1]))
            current = (current.astype(jnp.float32) + query_block.astype(jnp.float32) * filtered).astype(jnp.bfloat16)
        return current
    blocks = lax.map(one_block, jnp.arange(block_count, dtype=jnp.int32))
    return jnp.transpose(blocks, (1, 0, 2)).reshape(TOKENS, D)
```

```python
import jax
import jax.numpy as jnp
from jax import lax
from jax.experimental import pallas as pl
from jax.experimental.pallas import tpu as pltpu
from jax.sharding import PartitionSpec as P

D = 4096
EPS = 1e-06
ROWS = 128
WIDTH = 256
SEC = 4
CTX = 16
PEERS = 16
f32 = jnp.float32
bf16 = jnp.bfloat16


def shifted(value, axis, steps, wrap):
    count = lax.axis_size(axis)
    pairs = [
        (source, (source + steps) % count)
        for source in range(count)
        if wrap or 0 <= source + steps < count
    ]
    return lax.ppermute(value, axis, pairs)


def lanes_of(position):
    return pl.ds(pl.multiple_of(position * WIDTH, WIDTH), WIDTH)


def pack_kernel(x_ref, q_ref, k_ref, squares_ref, own_ref, *send_refs):
    sec = lax.axis_index("sec")
    x = x_ref[...].astype(f32)
    squared = x * x
    folded = squared[:, :128] + squared[:, 128:]
    squares = jnp.sum(folded.T, axis=0, keepdims=True)
    squares_ref[...] = jnp.broadcast_to(squares, squares_ref.shape)
    for distance, ref in enumerate((own_ref,) + send_refs):
        lanes = lanes_of(lax.rem(sec + distance, SEC))
        ref[0] = q_ref[0, :, lanes]
        ref[1] = k_ref[0, :, lanes]


def field_of(refs, section, which, rows=None):
    distance = lax.rem(lax.axis_index("sec") - section + SEC, SEC)

    def read(ref):
        part = ref[which] if rows is None else ref[which, rows]
        return part.astype(f32)

    chosen = read(refs[0])
    for index in range(1, SEC):
        chosen = jnp.where(distance == index, read(refs[index]), chosen)
    return chosen


def short_sum(padded_ref, taps):
    total = taps[0:1] * padded_ref[8 : 8 + ROWS]
    for tap in range(1, 7):
        total += taps[tap : tap + 1] * padded_ref[8 - tap : 8 - tap + ROWS]
    return total


def first_kernel(
    x_ref, squares_ref, gain_ref, taps_ref, f0, f1, f2, f3,
    head_ref, stream_ref, halo_ref, far_ref, pad_ref,
):
    fields = (f0, f1, f2, f3)
    lanes = lanes_of(lax.axis_index("sec"))
    sums = jnp.sum(squares_ref[...], axis=0, keepdims=True)
    inverse = lax.rsqrt(jnp.broadcast_to(sums, (128, 128)).T / D + EPS)
    inverse = jnp.concatenate([inverse, inverse], axis=1)
    stream = (x_ref[...].astype(f32) * inverse * gain_ref[:, lanes]).astype(bf16).astype(f32)
    gated = field_of(fields, 0, 1) * stream
    pad_ref[0:8] = jnp.zeros((8, WIDTH), f32)
    pad_ref[8:] = gated
    filtered = short_sum(pad_ref, taps_ref[0, :, lanes])
    q0 = field_of(fields, 0, 0)
    k1 = field_of(fields, 1, 1)
    raw = stream + q0 * filtered
    head_ref[...] = raw[0:8]
    rounded = raw.astype(bf16)
    stream_ref[...] = rounded
    rounded = rounded.astype(f32)
    halo_ref[0:8] = k1[0:8] * raw[0:8]
    halo_ref[8:ROWS] = k1[8:] * rounded[8:]
    halo_ref[ROWS : ROWS + 8] = gated[ROWS - 8 :]
    halo_ref[ROWS + 8 : ROWS + 16] = k1[0:8] * q0[0:8]
    far_ref[...] = gated[ROWS - 8 :]


def medium_part(source_ref, taps_ref, partial_ref, groups, first_source):
    low, high = groups

    def step(index, carry):
        shift = lax.rem(index, 8)
        column = index // 8
        here = pl.ds(pl.multiple_of(column * 128, 128), 128)
        taps = [
            jnp.broadcast_to(taps_ref[shift, a : a + 1, here], (8, 128)) for a in range(16)
        ]
        for group in range(low, high):
            total = None
            for a in range(16):
                origin = group - a
                if origin < first_source:
                    continue
                start = 8 * (origin - first_source)
                term = taps[a] * source_ref[start : start + 8, here]
                total = term if total is None else total + term
            start = 8 * (group - low)
            partial_ref[shift, start : start + 8, here] = total
        return carry

    lax.fori_loop(0, 16, step, 0)


def mode_rows(state, decays, weights, rows):
    position = lax.broadcasted_iota(jnp.int32, (8, WIDTH), 0)
    sums = jnp.zeros((8, WIDTH), f32)
    for row in range(8):
        state = decays * state
        if rows is not None:
            state = state + rows[row : row + 1]
        summed = jnp.sum(weights * state, axis=0, keepdims=True)
        sums = jnp.where(position == row, summed, sums)
    return state, sums


def second_kernel(
    own_ref, near_ref, far_ref, head_ref, stream_ref, short_ref, medium_ref,
    rates_ref, residues_ref, direct_ref, f0, f1, f2, f3,
    next_ref, gated_ref, ends_ref, tail_ref,
    source_ref, partial_ref, taps_ref, pad_ref,
):
    fields = (f0, f1, f2, f3)
    sec = lax.axis_index("sec")
    lanes = lanes_of(sec)
    taps = short_ref[0, :, lanes]

    def correction(before):
        pad_ref[0:8] = before
        pad_ref[8:16] = jnp.zeros((8, WIDTH), f32)
        total = jnp.zeros((8, WIDTH), f32)
        for tap in range(1, 7):
            total += taps[tap : tap + 1] * pad_ref[8 - tap : 16 - tap]
        return total

    head_q0 = field_of(fields, 0, 0, pl.ds(0, 16))[0:8]
    head_k1 = field_of(fields, 1, 1, pl.ds(0, 16))[0:8]
    mine = (head_ref[...] + head_q0 * correction(near_ref[ROWS : ROWS + 8])).astype(bf16).astype(f32)
    source_ref[0:8] = near_ref[0:8] + near_ref[ROWS + 8 : ROWS + 16] * correction(far_ref[...])
    source_ref[8:ROWS] = near_ref[8:ROWS]
    source_ref[ROWS : ROWS + 8] = head_k1 * mine
    source_ref[ROWS + 8 :] = own_ref[8:ROWS]
    medium_taps = medium_ref[:, lanes].reshape(16, 8, WIDTH)
    for shift in range(8):
        taps_ref[shift] = medium_taps[:, shift]
    medium_part(source_ref, taps_ref, partial_ref, (-1, 16), -16)
    filtered = partial_ref[0, 8 : 8 + ROWS]
    for shift in range(1, 8):
        filtered += partial_ref[shift, 8 - shift : 8 - shift + ROWS]
    stream = jnp.concatenate([mine, stream_ref[...].astype(f32)[8:]], axis=0)
    stream = (stream + field_of(fields, 1, 0) * filtered).astype(bf16)
    next_ref[...] = stream
    stream = stream.astype(f32)
    gated = field_of(fields, 2, 1) * stream
    gated_ref[...] = gated
    rates = rates_ref[:, lanes]
    decays = jnp.exp(-rates)
    weights = residues_ref[:, lanes] * jnp.sqrt(jnp.tanh(rates) * (1.0 + jnp.exp(-2.0 * rates)))

    def step(index, state):
        rows = gated_ref[pl.ds(pl.multiple_of(index * 8, 8), 8)]
        for row in range(8):
            state = decays * state + rows[row : row + 1]
        return state

    state = lax.fori_loop(0, ROWS // 8 - 1, step, jnp.zeros((8, WIDTH), f32))
    last = gated[ROWS - 8 :]
    state, sums = mode_rows(state, decays, weights, last)
    ends_ref[...] = jnp.broadcast_to(state[None], ends_ref.shape)
    q2 = field_of(fields, 2, 0, pl.ds(ROWS - 16, 16))[8:]
    k3 = field_of(fields, 3, 1, pl.ds(ROWS - 16, 16))[8:]
    tail_ref[0:8] = k3 * (stream[ROWS - 8 :] + q2 * (sums + direct_ref[:, lanes] * last))
    tail_ref[8:16] = k3 * q2


def third_kernel(
    gated_ref, stream_ref, ends_ref, tail_ref, short_ref,
    rates_ref, residues_ref, direct_ref, f0, f1, f2, f3,
    out_ref, sums_ref, pad_ref,
):
    fields = (f0, f1, f2, f3)
    lanes = lanes_of(lax.axis_index("sec"))
    mine = lax.axis_index("ctx")
    rates = rates_ref[:, lanes]
    decays = jnp.exp(-rates)
    weights = residues_ref[:, lanes] * jnp.sqrt(jnp.tanh(rates) * (1.0 + jnp.exp(-2.0 * rates)))
    span = jnp.exp(-rates * ROWS)
    state = jnp.zeros((8, WIDTH), f32)
    previous = state
    for position in range(CTX - 1):
        longer = span * state + ends_ref[position]
        previous = jnp.where(position < mine - 1, longer, previous)
        state = jnp.where(position < mine, longer, state)
    tail_state = jnp.exp(-rates * (ROWS - 8)) * previous
    _, carried = mode_rows(tail_state, decays, weights, None)
    pad_ref[0:8] = tail_ref[0:8] + tail_ref[8:16] * carried

    def step(index, state):
        here = pl.ds(pl.multiple_of(index * 8, 8), 8)
        state, sums = mode_rows(state, decays, weights, gated_ref[here])
        sums_ref[here] = sums
        return state

    lax.fori_loop(0, ROWS // 8, step, state)
    filtered = sums_ref[...] + direct_ref[:, lanes] * gated_ref[...]
    stream = stream_ref[...].astype(f32) + field_of(fields, 2, 0) * filtered
    stream = stream.astype(bf16).astype(f32)
    pad_ref[8:] = field_of(fields, 3, 1) * stream
    filtered = short_sum(pad_ref, short_ref[1, :, lanes])
    out_ref[...] = (stream + field_of(fields, 3, 0) * filtered).astype(bf16)


def shape(dims, dtype):
    return jax.ShapeDtypeStruct(dims, dtype)


def call(kernel, outs, scratch, operands, name, flops=1000000):
    vmem = pl.BlockSpec(memory_space=pltpu.VMEM)
    return pl.pallas_call(
        kernel,
        out_shape=outs,
        in_specs=[vmem] * len(operands),
        out_specs=[vmem] * len(outs),
        scratch_shapes=scratch,
        compiler_params=pltpu.CompilerParams(vmem_limit_bytes=32 * 1024 * 1024),
        cost_estimate=pl.CostEstimate(flops=flops, bytes_accessed=1000000, transcendentals=0),
        name=name,
    )(*operands)


def shards(x, q, k, gain, short, medium, rates, residues, direct):
    gain, direct = gain[None], direct[None]
    pair = shape((2, ROWS, WIDTH), bf16)
    squares, own, *sends = call(
        pack_kernel, [shape((PEERS, 128), f32)] + [pair] * 4, [], (x, q, k), "pack"
    )
    fields = [own] + [
        shifted(part, "sec", distance + 1, True) for distance, part in enumerate(sends)
    ]
    squares = lax.all_to_all(squares, ("sec", "ch"), 0, 0, tiled=True)
    head, stream, halo, far = call(
        first_kernel,
        [
            shape((8, WIDTH), f32),
            shape((ROWS, WIDTH), bf16),
            shape((ROWS + 16, WIDTH), f32),
            shape((8, WIDTH), f32),
        ],
        [pltpu.VMEM((ROWS + 8, WIDTH), f32)],
        (x, squares, gain, short, *fields),
        "first",
    )
    near_in = shifted(halo, "ctx", 1, False)
    far_in = shifted(far, "ctx", 2, False)
    stream, gated, ends, tail = call(
        second_kernel,
        [
            shape((ROWS, WIDTH), bf16),
            shape((ROWS, WIDTH), f32),
            shape((CTX, 8, WIDTH), f32),
            shape((16, WIDTH), f32),
        ],
        [
            pltpu.VMEM((2 * ROWS, WIDTH), f32),
            pltpu.VMEM((8, ROWS + 8, WIDTH), f32),
            pltpu.VMEM((8, 16, WIDTH), f32),
            pltpu.VMEM((16, WIDTH), f32),
        ],
        (halo, near_in, far_in, head, stream, short, medium, rates, residues, direct, *fields),
        "second",
    )
    tail_in = shifted(tail, "ctx", 1, False)
    ends = lax.all_to_all(ends, "ctx", 0, 0, tiled=True)
    (out,) = call(
        third_kernel,
        [shape((ROWS, WIDTH), bf16)],
        [pltpu.VMEM((ROWS, WIDTH), f32), pltpu.VMEM((ROWS + 8, WIDTH), f32)],
        (gated, stream, ends, tail_in, short, rates, residues, direct, *fields),
        "third",
    )
    return out


def solution(mesh):
    in_specs = (
        P("ctx", ("ch", "sec")),
        P("sec", "ctx", "ch"),
        P("sec", "ctx", "ch"),
        P("ch"),
        P(None, None, "ch"),
        P(None, "ch"),
        P(None, "ch"),
        P(None, "ch"),
        P("ch"),
    )
    out_specs = P("ctx", ("ch", "sec"))
    return jax.shard_map(shards, mesh=mesh, in_specs=in_specs, out_specs=out_specs, check_vma=False)
```

```python
import jax
import jax.numpy as jnp
from jax import lax
from jax.experimental import pallas as pl
from jax.experimental.pallas import tpu as pltpu
from jax.sharding import PartitionSpec as P

D = 4096
EPS = 1e-06
ROWS = 128
WIDTH = 256
SEC = 4
CTX = 16
PEERS = 16
f32 = jnp.float32
bf16 = jnp.bfloat16


def shifted(value, axis, steps, wrap):
    count = lax.axis_size(axis)
    pairs = [
        (source, (source + steps) % count)
        for source in range(count)
        if wrap or 0 <= source + steps < count
    ]
    return lax.ppermute(value, axis, pairs)


def lanes_of(position):
    return pl.ds(pl.multiple_of(position * WIDTH, WIDTH), WIDTH)


def squares_kernel(x_hbm, squares_ref, x_ref, sem):
    load = pltpu.make_async_copy(x_hbm, x_ref, sem)
    load.start()
    load.wait()
    x = x_ref[...].astype(f32)
    squared = x * x
    folded = squared[:, :128] + squared[:, 128:]
    squares = jnp.sum(folded.T, axis=0, keepdims=True)
    squares_ref[...] = jnp.broadcast_to(squares, squares_ref.shape)


def pack_kernel(after_ref, q_hbm, k_hbm, own_ref, send_1, send_2, send_3, sems):
    sec = lax.axis_index("sec")
    loads = []
    for distance, ref in enumerate((own_ref, send_1, send_2, send_3)):
        lanes = lanes_of(lax.rem(sec + distance, SEC))
        for which, source in enumerate((q_hbm, k_hbm)):
            loads.append(
                pltpu.make_async_copy(
                    source.at[0, :, lanes], ref.at[which], sems.at[2 * distance + which]
                )
            )
    for load in loads:
        load.start()
    for load in loads:
        load.wait()


def field_of(refs, section, which, rows=None):
    distance = lax.rem(lax.axis_index("sec") - section + SEC, SEC)

    def read(ref):
        part = ref[which] if rows is None else ref[which, rows]
        return part.astype(f32)

    chosen = read(refs[0])
    for index in range(1, SEC):
        chosen = jnp.where(distance == index, read(refs[index]), chosen)
    return chosen


def short_sum(padded_ref, taps):
    total = taps[0:1] * padded_ref[8 : 8 + ROWS]
    for tap in range(1, 7):
        total += taps[tap : tap + 1] * padded_ref[8 - tap : 8 - tap + ROWS]
    return total


def first_kernel(
    x_ref, squares_ref, gain_ref, taps_ref, f0, f1, f2, f3,
    head_ref, stream_ref, own_ref, halo_ref, far_ref, pad_ref,
):
    fields = (f0, f1, f2, f3)
    lanes = lanes_of(lax.axis_index("sec"))
    sums = jnp.sum(squares_ref[...], axis=0, keepdims=True)
    inverse = lax.rsqrt(jnp.broadcast_to(sums, (128, 128)).T / D + EPS)
    inverse = jnp.concatenate([inverse, inverse], axis=1)
    stream = (x_ref[...].astype(f32) * inverse * gain_ref[:, lanes]).astype(bf16).astype(f32)
    gated = field_of(fields, 0, 1) * stream
    pad_ref[0:8] = jnp.zeros((8, WIDTH), f32)
    pad_ref[8:] = gated
    filtered = short_sum(pad_ref, taps_ref[0, :, lanes])
    q0 = field_of(fields, 0, 0)
    k1 = field_of(fields, 1, 1)
    raw = stream + q0 * filtered
    head_ref[...] = raw[0:8]
    rounded = raw.astype(bf16)
    stream_ref[...] = rounded
    rounded = rounded.astype(f32)
    gated_1 = jnp.concatenate([k1[0:8] * raw[0:8], k1[8:] * rounded[8:]], axis=0)
    own_ref[...] = gated_1
    halo_ref[0:ROWS] = gated_1.astype(bf16)
    last = gated[ROWS - 8 :]
    gates = k1[0:8] * q0[0:8]
    halo_ref[ROWS : ROWS + 16] = jnp.concatenate([last, gates], axis=0).astype(bf16)
    last_rows = pl.ds(ROWS - 16, 16)
    halo_ref[ROWS + 16 :] = (
        field_of(fields, 2, 0, last_rows) * field_of(fields, 3, 1, last_rows)
    ).astype(bf16)
    far_ref[...] = jnp.concatenate([last, last], axis=0).astype(bf16)


def medium_part(source_ref, taps_ref, partial_ref, groups, first_source):
    low, high = groups

    def step(index, carry):
        shift = lax.rem(index, 8)
        column = index // 8
        here = pl.ds(pl.multiple_of(column * 128, 128), 128)
        taps = [
            jnp.broadcast_to(taps_ref[shift, a : a + 1, here], (8, 128)) for a in range(16)
        ]
        for group in range(low, high):
            total = None
            for a in range(16):
                origin = group - a
                if origin < first_source:
                    continue
                start = 8 * (origin - first_source)
                term = taps[a] * source_ref[start : start + 8, here]
                total = term if total is None else total + term
            start = 8 * (group - low)
            partial_ref[shift, start : start + 8, here] = total
        return carry

    lax.fori_loop(0, 16, step, 0)


def mode_rows(state, decays, weights, rows):
    position = lax.broadcasted_iota(jnp.int32, (8, WIDTH), 0)
    sums = jnp.zeros((8, WIDTH), f32)
    for row in range(8):
        state = decays * state
        if rows is not None:
            state = state + rows[row : row + 1]
        summed = jnp.sum(weights * state, axis=0, keepdims=True)
        sums = jnp.where(position == row, summed, sums)
    return state, sums


def second_kernel(
    own_ref, near_ref, far_ref, head_ref, stream_ref, short_ref, medium_ref,
    rates_ref, residues_ref, direct_ref, f0, f1, f2, f3,
    next_ref, gated_ref, ends_ref,
    source_ref, partial_ref, taps_ref, pad_ref,
):
    fields = (f0, f1, f2, f3)
    sec = lax.axis_index("sec")
    lanes = lanes_of(sec)
    taps = short_ref[0, :, lanes]

    def correction(before):
        pad_ref[0:8] = before
        pad_ref[8:16] = jnp.zeros((8, WIDTH), f32)
        total = jnp.zeros((8, WIDTH), f32)
        for tap in range(1, 7):
            total += taps[tap : tap + 1] * pad_ref[8 - tap : 16 - tap]
        return total

    head_q0 = field_of(fields, 0, 0, pl.ds(0, 16))[0:8]
    head_k1 = field_of(fields, 1, 1, pl.ds(0, 16))[0:8]
    joints = near_ref[ROWS : ROWS + 16].astype(f32)
    mine = (head_ref[...] + head_q0 * correction(joints[0:8])).astype(bf16).astype(f32)
    near = near_ref[0:ROWS].astype(f32)
    far = far_ref[...].astype(f32)
    source_ref[0:8] = near[0:8] + joints[8:16] * correction(far[0:8])
    source_ref[8:ROWS] = near[8:]
    source_ref[ROWS : ROWS + 8] = head_k1 * mine
    source_ref[ROWS + 8 :] = own_ref[8:ROWS]
    medium_taps = medium_ref[:, lanes].reshape(16, 8, WIDTH)
    for shift in range(8):
        taps_ref[shift] = medium_taps[:, shift]
    medium_part(source_ref, taps_ref, partial_ref, (-1, 16), -16)
    filtered = partial_ref[0, 8 : 8 + ROWS]
    for shift in range(1, 8):
        filtered += partial_ref[shift, 8 - shift : 8 - shift + ROWS]
    stream = jnp.concatenate([mine, stream_ref[...].astype(f32)[8:]], axis=0)
    stream = (stream + field_of(fields, 1, 0) * filtered).astype(bf16)
    next_ref[...] = stream
    stream = stream.astype(f32)
    gated = field_of(fields, 2, 1) * stream
    gated_ref[...] = gated
    rates = rates_ref[:, lanes]
    decays = jnp.exp(-rates)
    weights = residues_ref[:, lanes] * jnp.sqrt(jnp.tanh(rates) * (1.0 + jnp.exp(-2.0 * rates)))

    def step(index, state):
        rows = gated_ref[pl.ds(pl.multiple_of(index * 8, 8), 8)]
        for row in range(8):
            state = decays * state + rows[row : row + 1]
        return state

    state = lax.fori_loop(0, ROWS // 8 - 1, step, jnp.zeros((8, WIDTH), f32))
    last = gated[ROWS - 8 :]
    state, sums = mode_rows(state, decays, weights, last)
    q2 = field_of(fields, 2, 0, pl.ds(ROWS - 16, 16))[8:]
    k3 = field_of(fields, 3, 1, pl.ds(ROWS - 16, 16))[8:]
    tail = k3 * (stream[ROWS - 8 :] + q2 * (sums + direct_ref[:, lanes] * last))
    sent = jnp.concatenate([state, tail], axis=0).astype(bf16)
    ends_ref[...] = jnp.broadcast_to(sent[None], ends_ref.shape)


def third_kernel(
    gated_ref, stream_ref, ends_ref, near_ref, short_ref,
    rates_ref, residues_ref, direct_ref, f0, f1, f2, f3,
    out_ref, sums_ref, pad_ref,
):
    fields = (f0, f1, f2, f3)
    lanes = lanes_of(lax.axis_index("sec"))
    mine = lax.axis_index("ctx")
    rates = rates_ref[:, lanes]
    decays = jnp.exp(-rates)
    weights = residues_ref[:, lanes] * jnp.sqrt(jnp.tanh(rates) * (1.0 + jnp.exp(-2.0 * rates)))
    span = jnp.exp(-rates * ROWS)
    state = jnp.zeros((8, WIDTH), f32)
    previous = state
    tail = state
    for position in range(CTX - 1):
        received = ends_ref[position].astype(f32)
        longer = span * state + received[0:8]
        tail = jnp.where(position == mine - 1, received[8:16], tail)
        previous = jnp.where(position < mine - 1, longer, previous)
        state = jnp.where(position < mine, longer, state)
    tail_state = jnp.exp(-rates * (ROWS - 8)) * previous
    _, carried = mode_rows(tail_state, decays, weights, None)
    gates = near_ref[ROWS + 16 :].astype(f32)[8:]
    pad_ref[0:8] = tail + gates * carried

    def step(index, state):
        here = pl.ds(pl.multiple_of(index * 8, 8), 8)
        state, sums = mode_rows(state, decays, weights, gated_ref[here])
        sums_ref[here] = sums
        return state

    lax.fori_loop(0, ROWS // 8, step, state)
    filtered = sums_ref[...] + direct_ref[:, lanes] * gated_ref[...]
    stream = stream_ref[...].astype(f32) + field_of(fields, 2, 0) * filtered
    stream = stream.astype(bf16).astype(f32)
    pad_ref[8:] = field_of(fields, 3, 1) * stream
    filtered = short_sum(pad_ref, short_ref[1, :, lanes])
    out_ref[...] = (stream + field_of(fields, 3, 0) * filtered).astype(bf16)


def shape(dims, dtype):
    return jax.ShapeDtypeStruct(dims, dtype)


def call(kernel, outs, scratch, operands, name, in_hbm=(), flops=1000000, room=32):
    vmem = pl.BlockSpec(memory_space=pltpu.VMEM)
    return pl.pallas_call(
        kernel,
        out_shape=outs,
        in_specs=[
            pl.BlockSpec(memory_space=pltpu.HBM) if index in in_hbm else vmem
            for index in range(len(operands))
        ],
        out_specs=[vmem] * len(outs),
        scratch_shapes=scratch,
        compiler_params=pltpu.CompilerParams(vmem_limit_bytes=room * 1024 * 1024),
        cost_estimate=pl.CostEstimate(flops=flops, bytes_accessed=1000000, transcendentals=0),
        name=name,
    )(*operands)


def shards(x, q, k, gain, short, medium, rates, residues, direct):
    gain, direct = gain[None], direct[None]
    pair = shape((2, ROWS, WIDTH), bf16)
    (squares,) = call(
        squares_kernel,
        [shape((PEERS, 128), f32)],
        [pltpu.VMEM((ROWS, WIDTH), bf16), pltpu.SemaphoreType.DMA],
        (x,),
        "squares",
        in_hbm=(0,),
        room=60,
    )
    own, *sends = call(
        pack_kernel,
        [pair] * 4,
        [pltpu.SemaphoreType.DMA((8,))],
        (squares, q, k),
        "pack",
        in_hbm=(0, 1, 2),
        flops=10**11,
        room=60,
    )
    fields = [own] + [
        shifted(part, "sec", distance + 1, True) for distance, part in enumerate(sends)
    ]
    squares = lax.all_to_all(squares, ("sec", "ch"), 0, 0, tiled=True)
    head, stream, gated, halo, far = call(
        first_kernel,
        [
            shape((8, WIDTH), f32),
            shape((ROWS, WIDTH), bf16),
            shape((ROWS, WIDTH), f32),
            shape((ROWS + 32, WIDTH), bf16),
            shape((16, WIDTH), bf16),
        ],
        [pltpu.VMEM((ROWS + 8, WIDTH), f32)],
        (x, squares, gain, short, *fields),
        "first",
    )
    near_in = shifted(halo, "ctx", 1, False)
    far_in = shifted(far, "ctx", 2, False)
    stream, gated, ends = call(
        second_kernel,
        [
            shape((ROWS, WIDTH), bf16),
            shape((ROWS, WIDTH), f32),
            shape((CTX, 16, WIDTH), bf16),
        ],
        [
            pltpu.VMEM((2 * ROWS, WIDTH), f32),
            pltpu.VMEM((8, ROWS + 8, WIDTH), f32),
            pltpu.VMEM((8, 16, WIDTH), f32),
            pltpu.VMEM((16, WIDTH), f32),
        ],
        (gated, near_in, far_in, head, stream, short, medium, rates, residues, direct, *fields),
        "second",
    )
    ends = lax.all_to_all(ends, "ctx", 0, 0, tiled=True)
    (out,) = call(
        third_kernel,
        [shape((ROWS, WIDTH), bf16)],
        [pltpu.VMEM((ROWS, WIDTH), f32), pltpu.VMEM((ROWS + 8, WIDTH), f32)],
        (gated, stream, ends, near_in, short, rates, residues, direct, *fields),
        "third",
    )
    return out


def solution(mesh):
    in_specs = (
        P("ctx", ("ch", "sec")),
        P("sec", "ctx", "ch"),
        P("sec", "ctx", "ch"),
        P("ch"),
        P(None, None, "ch"),
        P(None, "ch"),
        P(None, "ch"),
        P(None, "ch"),
        P("ch"),
    )
    out_specs = P("ctx", ("ch", "sec"))
    return jax.shard_map(shards, mesh=mesh, in_specs=in_specs, out_specs=out_specs, check_vma=False)
```

```python
import jax
import jax.numpy as jnp
from jax import lax
from jax.experimental import pallas as pl
from jax.experimental.pallas import tpu as pltpu
from jax.sharding import PartitionSpec as P

D = 4096
EPS = 1e-06
ROWS = 128
WIDTH = 256
SEC = 4
CTX = 16
PEERS = 16
f32 = jnp.float32
bf16 = jnp.bfloat16


def shifted(value, axis, steps, wrap):
    count = lax.axis_size(axis)
    pairs = [
        (source, (source + steps) % count)
        for source in range(count)
        if wrap or 0 <= source + steps < count
    ]
    return lax.ppermute(value, axis, pairs)


def lanes_of(position):
    return pl.ds(pl.multiple_of(position * WIDTH, WIDTH), WIDTH)


def pack_kernel(x_hbm, q_hbm, k_hbm, squares_ref, own_ref, send_1, send_2, send_3, x_ref, sems):
    sec = lax.axis_index("sec")
    first = pltpu.make_async_copy(x_hbm, x_ref, sems.at[8])
    first.start()
    loads = []
    for distance, ref in enumerate((own_ref, send_1, send_2, send_3)):
        lanes = lanes_of(lax.rem(sec + distance, SEC))
        for which, source in enumerate((q_hbm, k_hbm)):
            loads.append(
                pltpu.make_async_copy(
                    source.at[0, :, lanes], ref.at[which], sems.at[2 * distance + which]
                )
            )
    for load in loads:
        load.start()
    first.wait()
    x = x_ref[...].astype(f32)
    squared = x * x
    folded = squared[:, :128] + squared[:, 128:]
    squares = jnp.sum(folded.T, axis=0, keepdims=True)
    squares_ref[...] = jnp.broadcast_to(squares, squares_ref.shape)
    for load in loads:
        load.wait()


def field_of(refs, section, which, rows=None):
    distance = lax.rem(lax.axis_index("sec") - section + SEC, SEC)

    def read(ref):
        part = ref[which] if rows is None else ref[which, rows]
        return part.astype(f32)

    chosen = read(refs[0])
    for index in range(1, SEC):
        chosen = jnp.where(distance == index, read(refs[index]), chosen)
    return chosen


def short_sum(padded_ref, taps):
    total = taps[0:1] * padded_ref[8 : 8 + ROWS]
    for tap in range(1, 7):
        total += taps[tap : tap + 1] * padded_ref[8 - tap : 8 - tap + ROWS]
    return total


def entry_kernel(x_ref, squares_ref, gain_ref, stream_ref):
    lanes = lanes_of(lax.axis_index("sec"))
    sums = jnp.sum(squares_ref[...], axis=0, keepdims=True)
    inverse = lax.rsqrt(jnp.broadcast_to(sums, (128, 128)).T / D + EPS)
    inverse = jnp.concatenate([inverse, inverse], axis=1)
    stream_ref[...] = (x_ref[...].astype(f32) * inverse * gain_ref[:, lanes]).astype(bf16)


def first_kernel(
    entry_ref, taps_ref, f0, f1, f2, f3,
    head_ref, stream_ref, own_ref, halo_ref, far_ref, pad_ref,
):
    fields = (f0, f1, f2, f3)
    lanes = lanes_of(lax.axis_index("sec"))
    stream = entry_ref[...].astype(f32)
    gated = field_of(fields, 0, 1) * stream
    pad_ref[0:8] = jnp.zeros((8, WIDTH), f32)
    pad_ref[8:] = gated
    filtered = short_sum(pad_ref, taps_ref[0, :, lanes])
    q0 = field_of(fields, 0, 0)
    k1 = field_of(fields, 1, 1)
    raw = stream + q0 * filtered
    head_ref[...] = raw[0:8]
    rounded = raw.astype(bf16)
    stream_ref[...] = rounded
    rounded = rounded.astype(f32)
    gated_1 = jnp.concatenate([k1[0:8] * raw[0:8], k1[8:] * rounded[8:]], axis=0)
    own_ref[...] = gated_1
    halo_ref[0:ROWS] = gated_1.astype(bf16)
    last = gated[ROWS - 8 :]
    gates = k1[0:8] * q0[0:8]
    halo_ref[ROWS : ROWS + 16] = jnp.concatenate([last, gates], axis=0).astype(bf16)
    last_rows = pl.ds(ROWS - 16, 16)
    halo_ref[ROWS + 16 :] = (
        field_of(fields, 2, 0, last_rows) * field_of(fields, 3, 1, last_rows)
    ).astype(bf16)
    far_ref[...] = jnp.concatenate([last, last], axis=0).astype(bf16)


def medium_part(source_ref, taps_ref, partial_ref, low, sources, earlier_ref=None):
    first, last = sources

    def step(index, carry):
        shift = lax.rem(index, 8)
        here = pl.ds(pl.multiple_of((index // 8) * 128, 128), 128)
        taps = [jnp.broadcast_to(taps_ref[shift, a : a + 1, here], (8, 128)) for a in range(16)]
        for group in range(low, 16):
            total = None
            if earlier_ref is not None and group >= 1:
                total = earlier_ref[shift, 8 * group - 8 : 8 * group, here]
            for a in range(16):
                origin = group - a
                if origin < first or origin > last:
                    continue
                start = 8 * (origin - first)
                term = taps[a] * source_ref[start : start + 8, here]
                total = term if total is None else total + term
            start = 8 * (group - low)
            partial_ref[shift, start : start + 8, here] = total
        return carry

    lax.fori_loop(0, 16, step, 0)


def own_kernel(
    gated_ref, medium_ref, rates_ref, residues_ref, partial_ref, taps_ref, powers_ref, carry_ref, kernel_ref
):
    lanes = lanes_of(lax.axis_index("sec"))
    medium_taps = medium_ref[:, lanes].reshape(16, 8, WIDTH)
    for shift in range(8):
        taps_ref[shift] = medium_taps[:, shift]
    medium_part(gated_ref.at[pl.ds(8, ROWS - 8)], taps_ref, partial_ref, 1, (1, 15))
    rates = rates_ref[:, lanes]
    weights = residues_ref[:, lanes] * jnp.sqrt(jnp.tanh(rates) * (1.0 + jnp.exp(-2.0 * rates)))
    position = lax.broadcasted_iota(jnp.int32, (8, WIDTH), 0)
    carries = []
    for age in range(9):
        power = jnp.exp(-rates * age)
        powers_ref[age] = power
        if age < 8:
            row = jnp.sum(weights * power, axis=0, keepdims=True)
            kernel_ref[age] = jnp.where(position >= age, row, 0.0)
        if age > 0:
            carries.append(weights * power)
    carries = jnp.stack(carries, axis=0)
    for mode in range(8):
        carry_ref[mode] = carries[:, mode]


def carried_rows(carry_ref, state):
    total = carry_ref[0] * state[0:1]
    for mode in range(1, 8):
        total += carry_ref[mode] * state[mode : mode + 1]
    return total


def within_rows(kernel_ref, rows, padded_ref):
    count = rows.shape[0]
    grouped = (count // 8, 8, WIDTH)
    total = rows.reshape(grouped) * kernel_ref[0][None]
    for age in range(1, 8):
        total += padded_ref[8 - age : 8 - age + count].reshape(grouped) * kernel_ref[age][None]
    return total.reshape(count, WIDTH)


def second_kernel(
    near_ref, far_ref, head_ref, stream_ref, short_ref,
    partial_ref, taps_ref, powers_ref, carry_ref, kernel_ref, direct_ref, f0, f1, f2, f3,
    next_ref, gated_ref, steps_ref, ends_ref, tail_ref,
    source_ref, sums_ref, pad_ref,
):
    fields = (f0, f1, f2, f3)
    lanes = lanes_of(lax.axis_index("sec"))
    taps = short_ref[0, :, lanes]

    def correction(before):
        pad_ref[0:8] = before
        pad_ref[8:16] = jnp.zeros((8, WIDTH), f32)
        total = jnp.zeros((8, WIDTH), f32)
        for tap in range(1, 7):
            total += taps[tap : tap + 1] * pad_ref[8 - tap : 16 - tap]
        return total

    head_q0 = field_of(fields, 0, 0, pl.ds(0, 16))[0:8]
    head_k1 = field_of(fields, 1, 1, pl.ds(0, 16))[0:8]
    joints = near_ref[ROWS : ROWS + 16].astype(f32)
    mine = (head_ref[...] + head_q0 * correction(joints[0:8])).astype(bf16).astype(f32)
    near = near_ref[0:ROWS].astype(f32)
    far = far_ref[...].astype(f32)
    source_ref[0:8] = near[0:8] + joints[8:16] * correction(far[0:8])
    source_ref[8:ROWS] = near[8:]
    source_ref[ROWS:] = head_k1 * mine
    medium_part(source_ref, taps_ref, sums_ref, -1, (-16, 0), partial_ref)
    filtered = sums_ref[0, 8 : 8 + ROWS]
    for shift in range(1, 8):
        filtered += sums_ref[shift, 8 - shift : 8 - shift + ROWS]
    stream = jnp.concatenate([mine, stream_ref[...].astype(f32)[8:]], axis=0)
    stream = (stream + field_of(fields, 1, 0) * filtered).astype(bf16)
    next_ref[...] = stream
    stream = stream.astype(f32)
    gated = field_of(fields, 2, 1) * stream
    gated_ref[...] = gated
    powers = [powers_ref[age] for age in range(9)]
    state = jnp.zeros((8, WIDTH), f32)
    before_last = state
    for group in range(16):
        step = powers[7] * gated[8 * group : 8 * group + 1]
        for row in range(1, 8):
            step += powers[7 - row] * gated[8 * group + row : 8 * group + row + 1]
        steps_ref[group] = step
        before_last = state
        state = powers[8] * state + step
    sent = jnp.concatenate([state[:, :128], state[:, 128:]], axis=0).astype(bf16)
    ends_ref[...] = jnp.broadcast_to(sent[None], ends_ref.shape)
    last = gated[ROWS - 8 :]
    pad_ref[8:16] = last
    sums = within_rows(kernel_ref, last, pad_ref) + carried_rows(carry_ref, before_last)
    q2 = field_of(fields, 2, 0, pl.ds(ROWS - 16, 16))[8:]
    k3 = field_of(fields, 3, 1, pl.ds(ROWS - 16, 16))[8:]
    tail_ref[...] = k3 * (stream[ROWS - 8 :] + q2 * (sums + direct_ref[:, lanes] * last))


def within_kernel(gated_ref, kernel_ref, direct_ref, local_ref, pad_ref):
    lanes = lanes_of(lax.axis_index("sec"))
    gated = gated_ref[...]
    pad_ref[0:8] = jnp.zeros((8, WIDTH), f32)
    pad_ref[8:] = gated
    local_ref[...] = within_rows(kernel_ref, gated, pad_ref) + direct_ref[:, lanes] * gated


def third_kernel(
    local_ref, steps_ref, stream_ref, ends_ref, tail_ref, near_ref, short_ref,
    rates_ref, powers_ref, carry_ref, f0, f1, f2, f3,
    out_ref, sums_ref, pad_ref,
):
    fields = (f0, f1, f2, f3)
    lanes = lanes_of(lax.axis_index("sec"))
    mine = lax.axis_index("ctx")
    rates = rates_ref[:, lanes]
    span = jnp.exp(-rates * ROWS)
    state = jnp.zeros((8, WIDTH), f32)
    previous = state
    for position in range(CTX - 1):
        received = ends_ref[position].astype(f32)
        longer = span * state + jnp.concatenate([received[0:8], received[8:16]], axis=1)
        previous = jnp.where(position < mine - 1, longer, previous)
        state = jnp.where(position < mine, longer, state)
    carried = carried_rows(carry_ref, jnp.exp(-rates * (ROWS - 8)) * previous)
    gates = near_ref[ROWS + 16 :].astype(f32)[8:]
    pad_ref[0:8] = tail_ref[...] + gates * carried
    for group in range(16):
        rows = slice(8 * group, 8 * group + 8)
        sums_ref[rows] = local_ref[rows] + carried_rows(carry_ref, state)
        state = powers_ref[8] * state + steps_ref[group]
    stream = stream_ref[...].astype(f32) + field_of(fields, 2, 0) * sums_ref[...]
    stream = stream.astype(bf16).astype(f32)
    pad_ref[8:] = field_of(fields, 3, 1) * stream
    filtered = short_sum(pad_ref, short_ref[1, :, lanes])
    out_ref[...] = (stream + field_of(fields, 3, 0) * filtered).astype(bf16)


def shape(dims, dtype):
    return jax.ShapeDtypeStruct(dims, dtype)


def call(kernel, outs, scratch, operands, name, in_hbm=(), flops=1000000, room=32):
    vmem = pl.BlockSpec(memory_space=pltpu.VMEM)
    return pl.pallas_call(
        kernel,
        out_shape=outs,
        in_specs=[
            pl.BlockSpec(memory_space=pltpu.HBM) if index in in_hbm else vmem
            for index in range(len(operands))
        ],
        out_specs=[vmem] * len(outs),
        scratch_shapes=scratch,
        compiler_params=pltpu.CompilerParams(vmem_limit_bytes=room * 1024 * 1024),
        cost_estimate=pl.CostEstimate(flops=flops, bytes_accessed=1000000, transcendentals=0),
        name=name,
    )(*operands)


def shards(x, q, k, gain, short, medium, rates, residues, direct):
    gain, direct = gain[None], direct[None]
    pair = shape((2, ROWS, WIDTH), bf16)
    squares, own, *sends = call(
        pack_kernel,
        [shape((PEERS, 128), f32)] + [pair] * 4,
        [pltpu.VMEM((ROWS, WIDTH), bf16), pltpu.SemaphoreType.DMA((9,))],
        (x, q, k),
        "pack",
        in_hbm=(0, 1, 2),
        room=60,
    )
    fields = [own] + [
        shifted(part, "sec", distance + 1, True) for distance, part in enumerate(sends)
    ]
    squares = lax.all_to_all(squares, ("sec", "ch"), 0, 0, tiled=True)
    (entry,) = call(
        entry_kernel, [shape((ROWS, WIDTH), bf16)], [], (x, squares, gain), "entry", flops=10**11
    )
    head, stream, gated, halo, far = call(
        first_kernel,
        [
            shape((8, WIDTH), f32),
            shape((ROWS, WIDTH), bf16),
            shape((ROWS, WIDTH), f32),
            shape((ROWS + 32, WIDTH), bf16),
            shape((16, WIDTH), bf16),
        ],
        [pltpu.VMEM((ROWS + 8, WIDTH), f32)],
        (entry, short, *fields),
        "first",
    )
    near_in = shifted(halo, "ctx", 1, False)
    far_in = shifted(far, "ctx", 2, False)
    table = shape((8, 8, WIDTH), f32)
    partial, taps, powers, carry, kernel = call(
        own_kernel,
        [
            shape((8, ROWS - 8, WIDTH), f32),
            shape((8, 16, WIDTH), f32),
            shape((9, 8, WIDTH), f32),
            table,
            table,
        ],
        [],
        (gated, medium, rates, residues),
        "own",
        flops=10**9,
    )
    stream, gated, steps, ends, tail = call(
        second_kernel,
        [
            shape((ROWS, WIDTH), bf16),
            shape((ROWS, WIDTH), f32),
            shape((16, 8, WIDTH), f32),
            shape((CTX, 16, 128), bf16),
            shape((8, WIDTH), f32),
        ],
        [
            pltpu.VMEM((ROWS + 8, WIDTH), f32),
            pltpu.VMEM((8, ROWS + 8, WIDTH), f32),
            pltpu.VMEM((16, WIDTH), f32),
        ],
        (near_in, far_in, head, stream, short, partial, taps, powers, carry, kernel, direct, *fields),
        "second",
    )
    tail_in = shifted(tail, "ctx", 1, False)
    ends = lax.all_to_all(ends, "ctx", 0, 0, tiled=True)
    (local,) = call(
        within_kernel,
        [shape((ROWS, WIDTH), f32)],
        [pltpu.VMEM((ROWS + 8, WIDTH), f32)],
        (gated, kernel, direct),
        "within",
        flops=10**9,
    )
    (out,) = call(
        third_kernel,
        [shape((ROWS, WIDTH), bf16)],
        [pltpu.VMEM((ROWS, WIDTH), f32), pltpu.VMEM((ROWS + 8, WIDTH), f32)],
        (local, steps, stream, ends, tail_in, near_in, short, rates, powers, carry, *fields),
        "third",
    )
    return out


def solution(mesh):
    in_specs = (
        P("ctx", ("ch", "sec")),
        P("sec", "ctx", "ch"),
        P("sec", "ctx", "ch"),
        P("ch"),
        P(None, None, "ch"),
        P(None, "ch"),
        P(None, "ch"),
        P(None, "ch"),
        P("ch"),
    )
    out_specs = P("ctx", ("ch", "sec"))
    return jax.shard_map(shards, mesh=mesh, in_specs=in_specs, out_specs=out_specs, check_vma=False)
```

```python
import jax
import jax.numpy as jnp
from jax import lax
from jax.experimental import pallas as pl
from jax.experimental.pallas import tpu as pltpu
from jax.sharding import PartitionSpec as P

D = 4096
EPS = 1e-06
ROWS = 128
WIDTH = 256
SEC = 4
CTX = 16
PEERS = 16
DISTANCES = (0, 2, 1, 3)
f32 = jnp.float32
bf16 = jnp.bfloat16


def shifted(value, axis, steps, wrap):
    count = lax.axis_size(axis)
    pairs = [
        (source, (source + steps) % count)
        for source in range(count)
        if wrap or 0 <= source + steps < count
    ]
    return lax.ppermute(value, axis, pairs)


def lanes_of(position):
    return pl.ds(pl.multiple_of(position * WIDTH, WIDTH), WIDTH)


def pack_kernel(x_hbm, q_hbm, k_hbm, squares_ref, own_ref, send_1, send_2, send_3, x_ref, sems):
    sec = lax.axis_index("sec")
    first = pltpu.make_async_copy(x_hbm, x_ref, sems.at[8])
    first.start()
    loads = []
    for slot, (distance, ref) in enumerate(zip(DISTANCES, (own_ref, send_1, send_2, send_3))):
        lanes = lanes_of(lax.rem(sec + distance, SEC))
        for which, source in enumerate((q_hbm, k_hbm)):
            loads.append(
                pltpu.make_async_copy(
                    source.at[0, :, lanes], ref.at[which], sems.at[2 * slot + which]
                )
            )
    for load in loads:
        load.start()
    first.wait()
    x = x_ref[...].astype(f32)
    squared = x * x
    folded = squared[:, :128] + squared[:, 128:]
    squares = jnp.sum(folded.T, axis=0, keepdims=True)
    squares_ref[...] = jnp.broadcast_to(squares, squares_ref.shape)
    for load in loads:
        load.wait()


def field_of(refs, section, which, rows=None):
    distance = lax.rem(lax.axis_index("sec") - section + SEC, SEC)

    def read(ref):
        part = ref[which] if rows is None else ref[which, rows]
        return part.astype(f32)

    chosen = read(refs[0])
    for index in range(1, SEC):
        chosen = jnp.where(distance == DISTANCES[index], read(refs[index]), chosen)
    return chosen


def short_sum(padded_ref, taps):
    total = taps[0:1] * padded_ref[8 : 8 + ROWS]
    for tap in range(1, 7):
        total += taps[tap : tap + 1] * padded_ref[8 - tap : 8 - tap + ROWS]
    return total


def entry_kernel(x_ref, squares_ref, gain_ref, stream_ref):
    lanes = lanes_of(lax.axis_index("sec"))
    sums = jnp.sum(squares_ref[...], axis=0, keepdims=True)
    inverse = lax.rsqrt(jnp.broadcast_to(sums, (128, 128)).T / D + EPS)
    inverse = jnp.concatenate([inverse, inverse], axis=1)
    stream_ref[...] = (x_ref[...].astype(f32) * inverse * gain_ref[:, lanes]).astype(bf16)


def first_kernel(
    entry_ref, taps_ref, f0, f1, f2, f3,
    head_ref, stream_ref, own_ref, halo_ref, far_ref, pad_ref,
):
    fields = (f0, f1, f2, f3)
    lanes = lanes_of(lax.axis_index("sec"))
    stream = entry_ref[...].astype(f32)
    gated = field_of(fields, 0, 1) * stream
    pad_ref[0:8] = jnp.zeros((8, WIDTH), f32)
    pad_ref[8:] = gated
    filtered = short_sum(pad_ref, taps_ref[0, :, lanes])
    q0 = field_of(fields, 0, 0)
    k1 = field_of(fields, 1, 1)
    raw = stream + q0 * filtered
    head_ref[...] = raw[0:8]
    rounded = raw.astype(bf16)
    stream_ref[...] = rounded
    rounded = rounded.astype(f32)
    gated_1 = jnp.concatenate([k1[0:8] * raw[0:8], k1[8:] * rounded[8:]], axis=0)
    own_ref[...] = gated_1
    halo_ref[0:ROWS] = gated_1.astype(bf16)
    last = gated[ROWS - 8 :]
    gates = k1[0:8] * q0[0:8]
    halo_ref[ROWS : ROWS + 16] = jnp.concatenate([last, gates], axis=0).astype(bf16)
    last_rows = pl.ds(ROWS - 16, 16)
    halo_ref[ROWS + 16 :] = (
        field_of(fields, 2, 0, last_rows) * field_of(fields, 3, 1, last_rows)
    ).astype(bf16)
    far_ref[...] = jnp.concatenate([last, last], axis=0).astype(bf16)


def medium_part(source_ref, taps_ref, partial_ref, low, sources, earlier_ref=None):
    first, last = sources

    def step(index, carry):
        shift = lax.rem(index, 8)
        here = pl.ds(pl.multiple_of((index // 8) * 128, 128), 128)
        taps = [jnp.broadcast_to(taps_ref[shift, a : a + 1, here], (8, 128)) for a in range(16)]
        for group in range(low, 16):
            total = None
            if earlier_ref is not None and group >= 1:
                total = earlier_ref[shift, 8 * group - 8 : 8 * group, here]
            for a in range(16):
                origin = group - a
                if origin < first or origin > last:
                    continue
                start = 8 * (origin - first)
                term = taps[a] * source_ref[start : start + 8, here]
                total = term if total is None else total + term
            start = 8 * (group - low)
            partial_ref[shift, start : start + 8, here] = total
        return carry

    lax.fori_loop(0, 16, step, 0)


def own_kernel(
    gated_ref, medium_ref, rates_ref, residues_ref, direct_ref,
    partial_ref, taps_ref, powers_ref, carry_ref, kernel_ref,
):
    lanes = lanes_of(lax.axis_index("sec"))
    medium_taps = medium_ref[:, lanes].reshape(16, 8, WIDTH)
    for shift in range(8):
        taps_ref[shift] = medium_taps[:, shift]
    medium_part(gated_ref.at[pl.ds(8, ROWS - 8)], taps_ref, partial_ref, 1, (1, 15))
    rates = rates_ref[:, lanes]
    weights = residues_ref[:, lanes] * jnp.sqrt(jnp.tanh(rates) * (1.0 + jnp.exp(-2.0 * rates)))
    position = lax.broadcasted_iota(jnp.int32, (8, WIDTH), 0)
    carries = []
    for age in range(9):
        power = jnp.exp(-rates * age)
        powers_ref[age] = power
        if age < 8:
            row = jnp.sum(weights * power, axis=0, keepdims=True)
            if age == 0:
                row += direct_ref[:, lanes]
            kernel_ref[age] = jnp.where(position >= age, row, 0.0)
        if age > 0:
            carries.append(weights * power)
    carries = jnp.stack(carries, axis=0)
    for mode in range(8):
        carry_ref[mode] = carries[:, mode]


def carried_rows(carry_ref, state):
    total = carry_ref[0] * state[0:1]
    for mode in range(1, 8):
        total += carry_ref[mode] * state[mode : mode + 1]
    return total


def within_rows(kernel_ref, rows, padded_ref):
    count = rows.shape[0]
    grouped = (count // 8, 8, WIDTH)
    total = rows.reshape(grouped) * kernel_ref[0][None]
    for age in range(1, 8):
        total += padded_ref[8 - age : 8 - age + count].reshape(grouped) * kernel_ref[age][None]
    return total.reshape(count, WIDTH)


def second_kernel(
    near_ref, far_ref, head_ref, stream_ref, short_ref,
    partial_ref, taps_ref, powers_ref, carry_ref, kernel_ref, f0, f1, f2, f3,
    next_ref, gated_ref, steps_ref, ends_ref, tail_ref,
    source_ref, sums_ref, pad_ref,
):
    fields = (f0, f1, f2, f3)
    lanes = lanes_of(lax.axis_index("sec"))
    taps = short_ref[0, :, lanes]

    def correction(before):
        pad_ref[0:8] = before
        pad_ref[8:16] = jnp.zeros((8, WIDTH), f32)
        total = jnp.zeros((8, WIDTH), f32)
        for tap in range(1, 7):
            total += taps[tap : tap + 1] * pad_ref[8 - tap : 16 - tap]
        return total

    head_q0 = field_of(fields, 0, 0, pl.ds(0, 16))[0:8]
    head_k1 = field_of(fields, 1, 1, pl.ds(0, 16))[0:8]
    joints = near_ref[ROWS : ROWS + 16].astype(f32)
    mine = (head_ref[...] + head_q0 * correction(joints[0:8])).astype(bf16).astype(f32)
    near = near_ref[0:ROWS].astype(f32)
    far = far_ref[...].astype(f32)
    source_ref[0:8] = near[0:8] + joints[8:16] * correction(far[0:8])
    source_ref[8:ROWS] = near[8:]
    source_ref[ROWS:] = head_k1 * mine
    medium_part(source_ref, taps_ref, sums_ref, -1, (-16, 0), partial_ref)
    filtered = sums_ref[0, 8 : 8 + ROWS]
    for shift in range(1, 8):
        filtered += sums_ref[shift, 8 - shift : 8 - shift + ROWS]
    stream = jnp.concatenate([mine, stream_ref[...].astype(f32)[8:]], axis=0)
    stream = (stream + field_of(fields, 1, 0) * filtered).astype(bf16)
    next_ref[...] = stream
    stream = stream.astype(f32)
    gated = field_of(fields, 2, 1) * stream
    gated_ref[...] = gated
    powers = [powers_ref[age] for age in range(9)]
    state = jnp.zeros((8, WIDTH), f32)
    before_last = state
    for group in range(16):
        step = powers[7] * gated[8 * group : 8 * group + 1]
        for row in range(1, 8):
            step += powers[7 - row] * gated[8 * group + row : 8 * group + row + 1]
        steps_ref[group] = step
        before_last = state
        state = powers[8] * state + step
    sent = jnp.concatenate([state[:, :128], state[:, 128:]], axis=0).astype(bf16)
    ends_ref[...] = jnp.broadcast_to(sent[None], ends_ref.shape)
    last = gated[ROWS - 8 :]
    pad_ref[8:16] = last
    sums = within_rows(kernel_ref, last, pad_ref) + carried_rows(carry_ref, before_last)
    q2 = field_of(fields, 2, 0, pl.ds(ROWS - 16, 16))[8:]
    k3 = field_of(fields, 3, 1, pl.ds(ROWS - 16, 16))[8:]
    tail_ref[...] = k3 * (stream[ROWS - 8 :] + q2 * sums)


def within_kernel(gated_ref, kernel_ref, local_ref, pad_ref):
    gated = gated_ref[...]
    pad_ref[0:8] = jnp.zeros((8, WIDTH), f32)
    pad_ref[8:] = gated
    local_ref[...] = within_rows(kernel_ref, gated, pad_ref)


def third_kernel(
    local_ref, steps_ref, stream_ref, ends_ref, tail_ref, near_ref, short_ref,
    rates_ref, powers_ref, carry_ref, f0, f1, f2, f3,
    out_ref, sums_ref, pad_ref,
):
    fields = (f0, f1, f2, f3)
    lanes = lanes_of(lax.axis_index("sec"))
    mine = lax.axis_index("ctx")
    rates = rates_ref[:, lanes]
    span = jnp.exp(-rates * ROWS)
    state = jnp.zeros((8, WIDTH), f32)
    previous = state
    for position in range(CTX - 1):
        received = ends_ref[position].astype(f32)
        longer = span * state + jnp.concatenate([received[0:8], received[8:16]], axis=1)
        previous = jnp.where(position < mine - 1, longer, previous)
        state = jnp.where(position < mine, longer, state)
    carried = carried_rows(carry_ref, jnp.exp(-rates * (ROWS - 8)) * previous)
    gates = near_ref[ROWS + 16 :].astype(f32)[8:]
    pad_ref[0:8] = tail_ref[...] + gates * carried
    for group in range(16):
        rows = slice(8 * group, 8 * group + 8)
        sums_ref[rows] = local_ref[rows] + carried_rows(carry_ref, state)
        state = powers_ref[8] * state + steps_ref[group]
    stream = stream_ref[...].astype(f32) + field_of(fields, 2, 0) * sums_ref[...]
    stream = stream.astype(bf16).astype(f32)
    pad_ref[8:] = field_of(fields, 3, 1) * stream
    filtered = short_sum(pad_ref, short_ref[1, :, lanes])
    out_ref[...] = (stream + field_of(fields, 3, 0) * filtered).astype(bf16)


def shape(dims, dtype):
    return jax.ShapeDtypeStruct(dims, dtype)


def call(kernel, outs, scratch, operands, name, in_hbm=(), flops=1000000, room=32):
    vmem = pl.BlockSpec(memory_space=pltpu.VMEM)
    return pl.pallas_call(
        kernel,
        out_shape=outs,
        in_specs=[
            pl.BlockSpec(memory_space=pltpu.HBM) if index in in_hbm else vmem
            for index in range(len(operands))
        ],
        out_specs=[vmem] * len(outs),
        scratch_shapes=scratch,
        compiler_params=pltpu.CompilerParams(vmem_limit_bytes=room * 1024 * 1024),
        cost_estimate=pl.CostEstimate(flops=flops, bytes_accessed=1000000, transcendentals=0),
        name=name,
    )(*operands)


def shards(x, q, k, gain, short, medium, rates, residues, direct):
    gain, direct = gain[None], direct[None]
    pair = shape((2, ROWS, WIDTH), bf16)
    squares, own, *sends = call(
        pack_kernel,
        [shape((PEERS, 128), f32)] + [pair] * 4,
        [pltpu.VMEM((ROWS, WIDTH), bf16), pltpu.SemaphoreType.DMA((9,))],
        (x, q, k),
        "pack",
        in_hbm=(0, 1, 2),
        room=60,
    )
    fields = [own] + [
        shifted(part, "sec", distance, True) for distance, part in zip(DISTANCES[1:], sends)
    ]
    squares = lax.all_to_all(squares, ("sec", "ch"), 0, 0, tiled=True)
    (entry,) = call(
        entry_kernel, [shape((ROWS, WIDTH), bf16)], [], (x, squares, gain), "entry", flops=10**11
    )
    head, stream, gated, halo, far = call(
        first_kernel,
        [
            shape((8, WIDTH), f32),
            shape((ROWS, WIDTH), bf16),
            shape((ROWS, WIDTH), f32),
            shape((ROWS + 32, WIDTH), bf16),
            shape((16, WIDTH), bf16),
        ],
        [pltpu.VMEM((ROWS + 8, WIDTH), f32)],
        (entry, short, *fields),
        "first",
    )
    near_in = shifted(halo, "ctx", 1, False)
    far_in = shifted(far, "ctx", 2, False)
    table = shape((8, 8, WIDTH), f32)
    partial, taps, powers, carry, kernel = call(
        own_kernel,
        [
            shape((8, ROWS - 8, WIDTH), f32),
            shape((8, 16, WIDTH), f32),
            shape((9, 8, WIDTH), f32),
            table,
            table,
        ],
        [],
        (gated, medium, rates, residues, direct),
        "own",
    )
    stream, gated, steps, ends, tail = call(
        second_kernel,
        [
            shape((ROWS, WIDTH), bf16),
            shape((ROWS, WIDTH), f32),
            shape((16, 8, WIDTH), f32),
            shape((CTX, 16, 128), bf16),
            shape((8, WIDTH), f32),
        ],
        [
            pltpu.VMEM((ROWS + 8, WIDTH), f32),
            pltpu.VMEM((8, ROWS + 8, WIDTH), f32),
            pltpu.VMEM((16, WIDTH), f32),
        ],
        (near_in, far_in, head, stream, short, partial, taps, powers, carry, kernel, *fields),
        "second",
    )
    tail_in = shifted(tail, "ctx", 1, False)
    ends = lax.all_to_all(ends, "ctx", 0, 0, tiled=True)
    (local,) = call(
        within_kernel,
        [shape((ROWS, WIDTH), f32)],
        [pltpu.VMEM((ROWS + 8, WIDTH), f32)],
        (gated, kernel),
        "within",
        flops=10**9,
    )
    (out,) = call(
        third_kernel,
        [shape((ROWS, WIDTH), bf16)],
        [pltpu.VMEM((ROWS, WIDTH), f32), pltpu.VMEM((ROWS + 8, WIDTH), f32)],
        (local, steps, stream, ends, tail_in, near_in, short, rates, powers, carry, *fields),
        "third",
    )
    return out


def solution(mesh):
    in_specs = (
        P("ctx", ("ch", "sec")),
        P("sec", "ctx", "ch"),
        P("sec", "ctx", "ch"),
        P("ch"),
        P(None, None, "ch"),
        P(None, "ch"),
        P(None, "ch"),
        P(None, "ch"),
        P("ch"),
    )
    out_specs = P("ctx", ("ch", "sec"))
    return jax.shard_map(shards, mesh=mesh, in_specs=in_specs, out_specs=out_specs, check_vma=False)
```

```python
import jax
import jax.numpy as jnp
from jax import lax
from jax.experimental import pallas as pl
from jax.experimental.pallas import tpu as pltpu
from jax.sharding import PartitionSpec as P

D = 4096
EPS = 1e-06
ROWS = 128
WIDTH = 256
SEC = 4
CTX = 16
PEERS = 16
DISTANCES = (0, 2, 1, 3)
f32 = jnp.float32
bf16 = jnp.bfloat16


def shifted(value, axis, steps, wrap):
    count = lax.axis_size(axis)
    pairs = [
        (source, (source + steps) % count)
        for source in range(count)
        if wrap or 0 <= source + steps < count
    ]
    return lax.ppermute(value, axis, pairs)


def lanes_of(position):
    return pl.ds(pl.multiple_of(position * WIDTH, WIDTH), WIDTH)


def pack_kernel(x_hbm, q_hbm, k_hbm, squares_ref, own_ref, send_1, send_2, send_3, x_ref, sems):
    sec = lax.axis_index("sec")
    first = pltpu.make_async_copy(x_hbm, x_ref, sems.at[8])
    first.start()
    loads = []
    for slot, (distance, ref) in enumerate(zip(DISTANCES, (own_ref, send_1, send_2, send_3))):
        lanes = lanes_of(lax.rem(sec + distance, SEC))
        for which, source in enumerate((q_hbm, k_hbm)):
            loads.append(
                pltpu.make_async_copy(
                    source.at[0, :, lanes], ref.at[which], sems.at[2 * slot + which]
                )
            )
    for load in loads:
        load.start()
    first.wait()
    x = x_ref[...].astype(f32)
    squared = x * x
    folded = squared[:, :128] + squared[:, 128:]
    squares = jnp.sum(folded.T, axis=0, keepdims=True)
    squares_ref[...] = jnp.broadcast_to(squares, squares_ref.shape)
    for load in loads:
        load.wait()


def field_of(refs, section, which, rows=None):
    distance = lax.rem(lax.axis_index("sec") - section + SEC, SEC)

    def read(ref):
        part = ref[which] if rows is None else ref[which, rows]
        return part.astype(f32)

    chosen = read(refs[0])
    for index in range(1, SEC):
        chosen = jnp.where(distance == DISTANCES[index], read(refs[index]), chosen)
    return chosen


def short_sum(padded_ref, taps):
    total = taps[0:1] * padded_ref[8 : 8 + ROWS]
    for tap in range(1, 7):
        total += taps[tap : tap + 1] * padded_ref[8 - tap : 8 - tap + ROWS]
    return total


def entry_kernel(x_ref, squares_ref, gain_ref, across_ref, kept_ref, stream_ref):
    lanes = lanes_of(lax.axis_index("sec"))
    sums = jnp.sum(squares_ref[...], axis=0, keepdims=True)
    inverse = lax.rsqrt(jnp.broadcast_to(sums, (128, 128)).T / D + EPS)
    inverse = jnp.concatenate([inverse, inverse], axis=1)
    stream_ref[...] = (x_ref[...].astype(f32) * inverse * gain_ref[:, lanes]).astype(bf16)


def first_kernel(
    entry_ref, taps_ref, f0, f1, f2, f3,
    head_ref, stream_ref, own_ref, halo_ref, far_ref, pad_ref,
):
    fields = (f0, f1, f2, f3)
    lanes = lanes_of(lax.axis_index("sec"))
    stream = entry_ref[...].astype(f32)
    gated = field_of(fields, 0, 1) * stream
    pad_ref[0:8] = jnp.zeros((8, WIDTH), f32)
    pad_ref[8:] = gated
    filtered = short_sum(pad_ref, taps_ref[0, :, lanes])
    q0 = field_of(fields, 0, 0)
    k1 = field_of(fields, 1, 1)
    raw = stream + q0 * filtered
    head_ref[...] = raw[0:8]
    rounded = raw.astype(bf16)
    stream_ref[...] = rounded
    rounded = rounded.astype(f32)
    gated_1 = jnp.concatenate([k1[0:8] * raw[0:8], k1[8:] * rounded[8:]], axis=0)
    own_ref[...] = gated_1
    halo_ref[0:ROWS] = gated_1.astype(bf16)
    last = gated[ROWS - 8 :]
    gates = k1[0:8] * q0[0:8]
    halo_ref[ROWS : ROWS + 16] = jnp.concatenate([last, gates], axis=0).astype(bf16)
    last_rows = pl.ds(ROWS - 16, 16)
    halo_ref[ROWS + 16 :] = (
        field_of(fields, 2, 0, last_rows) * field_of(fields, 3, 1, last_rows)
    ).astype(bf16)
    far_ref[...] = jnp.concatenate([last, last], axis=0).astype(bf16)


def medium_part(source_ref, taps_ref, partial_ref, low, sources, earlier_ref=None):
    first, last = sources

    def step(index, carry):
        shift = lax.rem(index, 8)
        here = pl.ds(pl.multiple_of((index // 8) * 128, 128), 128)
        taps = [jnp.broadcast_to(taps_ref[shift, a : a + 1, here], (8, 128)) for a in range(16)]
        for group in range(low, 16):
            total = None
            if earlier_ref is not None and group >= 1:
                total = earlier_ref[shift, 8 * group - 8 : 8 * group, here]
            for a in range(16):
                origin = group - a
                if origin < first or origin > last:
                    continue
                start = 8 * (origin - first)
                term = taps[a] * source_ref[start : start + 8, here]
                total = term if total is None else total + term
            start = 8 * (group - low)
            partial_ref[shift, start : start + 8, here] = total
        return carry

    lax.fori_loop(0, 16, step, 0)


def own_kernel(
    gated_ref, medium_ref, rates_ref, residues_ref, direct_ref,
    partial_ref, taps_ref, powers_ref, carry_ref, kernel_ref,
):
    lanes = lanes_of(lax.axis_index("sec"))
    medium_taps = medium_ref[:, lanes].reshape(16, 8, WIDTH)
    for shift in range(8):
        taps_ref[shift] = medium_taps[:, shift]
    medium_part(gated_ref.at[pl.ds(8, ROWS - 8)], taps_ref, partial_ref, 1, (1, 15))
    rates = rates_ref[:, lanes]
    weights = residues_ref[:, lanes] * jnp.sqrt(jnp.tanh(rates) * (1.0 + jnp.exp(-2.0 * rates)))
    position = lax.broadcasted_iota(jnp.int32, (8, WIDTH), 0)
    carries = []
    for age in range(9):
        power = jnp.exp(-rates * age)
        powers_ref[age] = power
        if age < 8:
            row = jnp.sum(weights * power, axis=0, keepdims=True)
            if age == 0:
                row += direct_ref[:, lanes]
            kernel_ref[age] = jnp.where(position >= age, row, 0.0)
        if age > 0:
            carries.append(weights * power)
    carries = jnp.stack(carries, axis=0)
    for mode in range(8):
        carry_ref[mode] = carries[:, mode]


def carried_rows(carry_ref, state):
    total = carry_ref[0] * state[0:1]
    for mode in range(1, 8):
        total += carry_ref[mode] * state[mode : mode + 1]
    return total


def within_rows(kernel_ref, rows, padded_ref):
    count = rows.shape[0]
    grouped = (count // 8, 8, WIDTH)
    total = rows.reshape(grouped) * kernel_ref[0][None]
    for age in range(1, 8):
        total += padded_ref[8 - age : 8 - age + count].reshape(grouped) * kernel_ref[age][None]
    return total.reshape(count, WIDTH)


def second_kernel(
    near_ref, far_ref, head_ref, stream_ref, short_ref,
    partial_ref, taps_ref, powers_ref, carry_ref, kernel_ref, f0, f1, f2, f3,
    next_ref, gated_ref, steps_ref, ends_ref, tail_ref,
    source_ref, sums_ref, pad_ref,
):
    fields = (f0, f1, f2, f3)
    lanes = lanes_of(lax.axis_index("sec"))
    taps = short_ref[0, :, lanes]

    def correction(before):
        pad_ref[0:8] = before
        pad_ref[8:16] = jnp.zeros((8, WIDTH), f32)
        total = jnp.zeros((8, WIDTH), f32)
        for tap in range(1, 7):
            total += taps[tap : tap + 1] * pad_ref[8 - tap : 16 - tap]
        return total

    head_q0 = field_of(fields, 0, 0, pl.ds(0, 16))[0:8]
    head_k1 = field_of(fields, 1, 1, pl.ds(0, 16))[0:8]
    joints = near_ref[ROWS : ROWS + 16].astype(f32)
    mine = (head_ref[...] + head_q0 * correction(joints[0:8])).astype(bf16).astype(f32)
    near = near_ref[0:ROWS].astype(f32)
    far = far_ref[...].astype(f32)
    source_ref[0:8] = near[0:8] + joints[8:16] * correction(far[0:8])
    source_ref[8:ROWS] = near[8:]
    source_ref[ROWS:] = head_k1 * mine
    medium_part(source_ref, taps_ref, sums_ref, -1, (-16, 0), partial_ref)
    filtered = sums_ref[0, 8 : 8 + ROWS]
    for shift in range(1, 8):
        filtered += sums_ref[shift, 8 - shift : 8 - shift + ROWS]
    stream = jnp.concatenate([mine, stream_ref[...].astype(f32)[8:]], axis=0)
    stream = (stream + field_of(fields, 1, 0) * filtered).astype(bf16)
    next_ref[...] = stream
    stream = stream.astype(f32)
    gated = field_of(fields, 2, 1) * stream
    gated_ref[...] = gated
    powers = [powers_ref[age] for age in range(9)]
    state = jnp.zeros((8, WIDTH), f32)
    before_last = state
    for group in range(16):
        step = powers[7] * gated[8 * group : 8 * group + 1]
        for row in range(1, 8):
            step += powers[7 - row] * gated[8 * group + row : 8 * group + row + 1]
        steps_ref[group] = step
        before_last = state
        state = powers[8] * state + step
    sent = jnp.concatenate([state[:, :128], state[:, 128:]], axis=0).astype(bf16)
    ends_ref[...] = jnp.broadcast_to(sent[None], ends_ref.shape)
    last = gated[ROWS - 8 :]
    pad_ref[8:16] = last
    sums = within_rows(kernel_ref, last, pad_ref) + carried_rows(carry_ref, before_last)
    q2 = field_of(fields, 2, 0, pl.ds(ROWS - 16, 16))[8:]
    k3 = field_of(fields, 3, 1, pl.ds(ROWS - 16, 16))[8:]
    tail_ref[...] = k3 * (stream[ROWS - 8 :] + q2 * sums)


def within_kernel(gated_ref, kernel_ref, local_ref, pad_ref):
    gated = gated_ref[...]
    pad_ref[0:8] = jnp.zeros((8, WIDTH), f32)
    pad_ref[8:] = gated
    local_ref[...] = within_rows(kernel_ref, gated, pad_ref)


def third_kernel(
    local_ref, steps_ref, stream_ref, ends_ref, tail_ref, near_ref, short_ref,
    rates_ref, powers_ref, carry_ref, f0, f1, f2, f3,
    out_ref, sums_ref, pad_ref,
):
    fields = (f0, f1, f2, f3)
    lanes = lanes_of(lax.axis_index("sec"))
    mine = lax.axis_index("ctx")
    rates = rates_ref[:, lanes]
    span = jnp.exp(-rates * ROWS)
    state = jnp.zeros((8, WIDTH), f32)
    previous = state
    for position in range(CTX - 1):
        received = ends_ref[position].astype(f32)
        longer = span * state + jnp.concatenate([received[0:8], received[8:16]], axis=1)
        previous = jnp.where(position < mine - 1, longer, previous)
        state = jnp.where(position < mine, longer, state)
    carried = carried_rows(carry_ref, jnp.exp(-rates * (ROWS - 8)) * previous)
    gates = near_ref[ROWS + 16 :].astype(f32)[8:]
    pad_ref[0:8] = tail_ref[...] + gates * carried
    for group in range(16):
        rows = slice(8 * group, 8 * group + 8)
        sums_ref[rows] = local_ref[rows] + carried_rows(carry_ref, state)
        state = powers_ref[8] * state + steps_ref[group]
    stream = stream_ref[...].astype(f32) + field_of(fields, 2, 0) * sums_ref[...]
    stream = stream.astype(bf16).astype(f32)
    pad_ref[8:] = field_of(fields, 3, 1) * stream
    filtered = short_sum(pad_ref, short_ref[1, :, lanes])
    out_ref[...] = (stream + field_of(fields, 3, 0) * filtered).astype(bf16)


def shape(dims, dtype):
    return jax.ShapeDtypeStruct(dims, dtype)


def call(kernel, outs, scratch, operands, name, in_hbm=(), flops=1000000, room=32):
    vmem = pl.BlockSpec(memory_space=pltpu.VMEM)
    return pl.pallas_call(
        kernel,
        out_shape=outs,
        in_specs=[
            pl.BlockSpec(memory_space=pl.ANY) if index in in_hbm else vmem
            for index in range(len(operands))
        ],
        out_specs=[vmem] * len(outs),
        scratch_shapes=scratch,
        compiler_params=pltpu.CompilerParams(vmem_limit_bytes=room * 1024 * 1024),
        cost_estimate=pl.CostEstimate(flops=flops, bytes_accessed=1000000, transcendentals=0),
        name=name,
    )(*operands)


def shards(x, q, k, gain, short, medium, rates, residues, direct):
    gain, direct = gain[None], direct[None]
    pair = shape((2, ROWS, WIDTH), bf16)
    squares, own, *sends = call(
        pack_kernel,
        [shape((PEERS, 128), f32)] + [pair] * 4,
        [pltpu.VMEM((ROWS, WIDTH), bf16), pltpu.SemaphoreType.DMA((9,))],
        (x, q, k),
        "pack",
        in_hbm=(0, 1, 2),
        room=60,
    )
    fields = [own] + [
        shifted(part, "sec", distance, True) for distance, part in zip(DISTANCES[1:], sends)
    ]
    squares = lax.all_to_all(squares, ("sec", "ch"), 0, 0, tiled=True)
    (entry,) = call(
        entry_kernel, [shape((ROWS, WIDTH), bf16)], [], (x, squares, gain, fields[1], own), "entry", in_hbm=(3,), flops=10**10
    )
    head, stream, gated, halo, far = call(
        first_kernel,
        [
            shape((8, WIDTH), f32),
            shape((ROWS, WIDTH), bf16),
            shape((ROWS, WIDTH), f32),
            shape((ROWS + 32, WIDTH), bf16),
            shape((16, WIDTH), bf16),
        ],
        [pltpu.VMEM((ROWS + 8, WIDTH), f32)],
        (entry, short, *fields),
        "first",
    )
    near_in = shifted(halo, "ctx", 1, False)
    far_in = shifted(far, "ctx", 2, False)
    table = shape((8, 8, WIDTH), f32)
    partial, taps, powers, carry, kernel = call(
        own_kernel,
        [
            shape((8, ROWS - 8, WIDTH), f32),
            shape((8, 16, WIDTH), f32),
            shape((9, 8, WIDTH), f32),
            table,
            table,
        ],
        [],
        (gated, medium, rates, residues, direct),
        "own",
    )
    stream, gated, steps, ends, tail = call(
        second_kernel,
        [
            shape((ROWS, WIDTH), bf16),
            shape((ROWS, WIDTH), f32),
            shape((16, 8, WIDTH), f32),
            shape((CTX, 16, 128), bf16),
            shape((8, WIDTH), f32),
        ],
        [
            pltpu.VMEM((ROWS + 8, WIDTH), f32),
            pltpu.VMEM((8, ROWS + 8, WIDTH), f32),
            pltpu.VMEM((16, WIDTH), f32),
        ],
        (near_in, far_in, head, stream, short, partial, taps, powers, carry, kernel, *fields),
        "second",
    )
    tail_in = shifted(tail, "ctx", 1, False)
    ends = lax.all_to_all(ends, "ctx", 0, 0, tiled=True)
    (local,) = call(
        within_kernel,
        [shape((ROWS, WIDTH), f32)],
        [pltpu.VMEM((ROWS + 8, WIDTH), f32)],
        (gated, kernel),
        "within",
        flops=10**9,
    )
    (out,) = call(
        third_kernel,
        [shape((ROWS, WIDTH), bf16)],
        [pltpu.VMEM((ROWS, WIDTH), f32), pltpu.VMEM((ROWS + 8, WIDTH), f32)],
        (local, steps, stream, ends, tail_in, near_in, short, rates, powers, carry, *fields),
        "third",
    )
    return out


def solution(mesh):
    in_specs = (
        P("ctx", ("ch", "sec")),
        P("sec", "ctx", "ch"),
        P("sec", "ctx", "ch"),
        P("ch"),
        P(None, None, "ch"),
        P(None, "ch"),
        P(None, "ch"),
        P(None, "ch"),
        P("ch"),
    )
    out_specs = P("ctx", ("ch", "sec"))
    return jax.shard_map(shards, mesh=mesh, in_specs=in_specs, out_specs=out_specs, check_vma=False)
```

```python
import jax
import jax.numpy as jnp
from jax import lax
from jax.experimental import pallas as pl
from jax.experimental.pallas import tpu as pltpu
from jax.sharding import PartitionSpec as P

D = 4096
EPS = 1e-06
ROWS = 128
WIDTH = 256
SEC = 4
CTX = 16
PEERS = 16
DISTANCES = (0, 2, 1, 3)
f32 = jnp.float32
bf16 = jnp.bfloat16


def shifted(value, axis, steps, wrap):
    count = lax.axis_size(axis)
    pairs = [
        (source, (source + steps) % count)
        for source in range(count)
        if wrap or 0 <= source + steps < count
    ]
    return lax.ppermute(value, axis, pairs)


def lanes_of(position):
    return pl.ds(pl.multiple_of(position * WIDTH, WIDTH), WIDTH)


def pack_kernel(x_hbm, q_hbm, k_hbm, squares_hbm, own_ref, send_1, send_2, send_3, x_ref, squares_ref, sems):
    sec = lax.axis_index("sec")
    first = pltpu.make_async_copy(x_hbm, x_ref, sems.at[8])
    first.start()
    loads = []
    for slot, (distance, ref) in enumerate(zip(DISTANCES, (own_ref, send_1, send_2, send_3))):
        lanes = lanes_of(lax.rem(sec + distance, SEC))
        for which, source in enumerate((q_hbm, k_hbm)):
            loads.append(
                pltpu.make_async_copy(
                    source.at[0, :, lanes], ref.at[which], sems.at[2 * slot + which]
                )
            )
    for load in loads:
        load.start()
    first.wait()
    x = x_ref[...].astype(f32)
    squared = x * x
    folded = squared[:, :128] + squared[:, 128:]
    squares = jnp.sum(folded.T, axis=0, keepdims=True)
    squares_ref[...] = jnp.broadcast_to(squares, squares_ref.shape)
    loads.append(pltpu.make_async_copy(squares_ref, squares_hbm, sems.at[9]))
    loads[-1].start()
    for load in loads:
        load.wait()


def field_of(refs, section, which, rows=None):
    distance = lax.rem(lax.axis_index("sec") - section + SEC, SEC)

    def read(ref):
        part = ref[which] if rows is None else ref[which, rows]
        return part.astype(f32)

    chosen = read(refs[0])
    for index in range(1, SEC):
        chosen = jnp.where(distance == DISTANCES[index], read(refs[index]), chosen)
    return chosen


def short_sum(padded_ref, taps):
    total = taps[0:1] * padded_ref[8 : 8 + ROWS]
    for tap in range(1, 7):
        total += taps[tap : tap + 1] * padded_ref[8 - tap : 8 - tap + ROWS]
    return total


def entry_kernel(x_ref, squares_ref, gain_ref, across_ref, kept_ref, stream_ref):
    lanes = lanes_of(lax.axis_index("sec"))
    sums = jnp.sum(squares_ref[...], axis=0, keepdims=True)
    inverse = lax.rsqrt(jnp.broadcast_to(sums, (128, 128)).T / D + EPS)
    inverse = jnp.concatenate([inverse, inverse], axis=1)
    stream_ref[...] = (x_ref[...].astype(f32) * inverse * gain_ref[:, lanes]).astype(bf16)


def first_kernel(
    entry_ref, taps_ref, f0, f1, f2, f3,
    head_ref, stream_ref, own_ref, halo_ref, far_ref, pad_ref,
):
    fields = (f0, f1, f2, f3)
    lanes = lanes_of(lax.axis_index("sec"))
    stream = entry_ref[...].astype(f32)
    gated = field_of(fields, 0, 1) * stream
    pad_ref[0:8] = jnp.zeros((8, WIDTH), f32)
    pad_ref[8:] = gated
    filtered = short_sum(pad_ref, taps_ref[0, :, lanes])
    q0 = field_of(fields, 0, 0)
    k1 = field_of(fields, 1, 1)
    raw = stream + q0 * filtered
    head_ref[...] = raw[0:8]
    rounded = raw.astype(bf16)
    stream_ref[...] = rounded
    rounded = rounded.astype(f32)
    gated_1 = jnp.concatenate([k1[0:8] * raw[0:8], k1[8:] * rounded[8:]], axis=0)
    own_ref[...] = gated_1
    halo_ref[0:ROWS] = gated_1.astype(bf16)
    last = gated[ROWS - 8 :]
    gates = k1[0:8] * q0[0:8]
    halo_ref[ROWS : ROWS + 16] = jnp.concatenate([last, gates], axis=0).astype(bf16)
    last_rows = pl.ds(ROWS - 16, 16)
    halo_ref[ROWS + 16 :] = (
        field_of(fields, 2, 0, last_rows) * field_of(fields, 3, 1, last_rows)
    ).astype(bf16)
    far_ref[...] = jnp.concatenate([last, last], axis=0).astype(bf16)


def medium_part(source_ref, taps_ref, partial_ref, low, sources, earlier_ref=None):
    first, last = sources

    def step(index, carry):
        shift = lax.rem(index, 8)
        here = pl.ds(pl.multiple_of((index // 8) * 128, 128), 128)
        taps = [jnp.broadcast_to(taps_ref[shift, a : a + 1, here], (8, 128)) for a in range(16)]
        for group in range(low, 16):
            total = None
            if earlier_ref is not None and group >= 1:
                total = earlier_ref[shift, 8 * group - 8 : 8 * group, here]
            for a in range(16):
                origin = group - a
                if origin < first or origin > last:
                    continue
                start = 8 * (origin - first)
                term = taps[a] * source_ref[start : start + 8, here]
                total = term if total is None else total + term
            start = 8 * (group - low)
            partial_ref[shift, start : start + 8, here] = total
        return carry

    lax.fori_loop(0, 16, step, 0, unroll=2)


def own_kernel(
    gated_ref, medium_ref, rates_ref, residues_ref, direct_ref,
    partial_ref, taps_ref, powers_ref, carry_ref, kernel_ref,
):
    lanes = lanes_of(lax.axis_index("sec"))
    medium_taps = medium_ref[:, lanes].reshape(16, 8, WIDTH)
    for shift in range(8):
        taps_ref[shift] = medium_taps[:, shift]
    medium_part(gated_ref.at[pl.ds(8, ROWS - 8)], taps_ref, partial_ref, 1, (1, 15))
    rates = rates_ref[:, lanes]
    weights = residues_ref[:, lanes] * jnp.sqrt(jnp.tanh(rates) * (1.0 + jnp.exp(-2.0 * rates)))
    position = lax.broadcasted_iota(jnp.int32, (8, WIDTH), 0)
    carries = []
    for age in range(9):
        power = jnp.exp(-rates * age)
        powers_ref[age] = power
        if age < 8:
            row = jnp.sum(weights * power, axis=0, keepdims=True)
            if age == 0:
                row += direct_ref[:, lanes]
            kernel_ref[age] = jnp.where(position >= age, row, 0.0)
        if age > 0:
            carries.append(weights * power)
    carries = jnp.stack(carries, axis=0)
    for mode in range(8):
        carry_ref[mode] = carries[:, mode]


def carried_rows(carry_ref, state):
    total = carry_ref[0] * state[0:1]
    for mode in range(1, 8):
        total += carry_ref[mode] * state[mode : mode + 1]
    return total


def within_rows(kernel_ref, rows, padded_ref):
    count = rows.shape[0]
    grouped = (count // 8, 8, WIDTH)
    total = rows.reshape(grouped) * kernel_ref[0][None]
    for age in range(1, 8):
        total += padded_ref[8 - age : 8 - age + count].reshape(grouped) * kernel_ref[age][None]
    return total.reshape(count, WIDTH)


def second_kernel(
    near_ref, far_ref, head_ref, stream_ref, short_ref,
    partial_ref, taps_ref, powers_ref, carry_ref, kernel_ref, f0, f1, f2, f3,
    next_ref, gated_ref, steps_ref, ends_ref, tail_ref,
    source_ref, sums_ref, pad_ref,
):
    fields = (f0, f1, f2, f3)
    lanes = lanes_of(lax.axis_index("sec"))
    taps = short_ref[0, :, lanes]

    def correction(before):
        pad_ref[0:8] = before
        pad_ref[8:16] = jnp.zeros((8, WIDTH), f32)
        total = jnp.zeros((8, WIDTH), f32)
        for tap in range(1, 7):
            total += taps[tap : tap + 1] * pad_ref[8 - tap : 16 - tap]
        return total

    head_q0 = field_of(fields, 0, 0, pl.ds(0, 16))[0:8]
    head_k1 = field_of(fields, 1, 1, pl.ds(0, 16))[0:8]
    joints = near_ref[ROWS : ROWS + 16].astype(f32)
    mine = (head_ref[...] + head_q0 * correction(joints[0:8])).astype(bf16).astype(f32)
    near = near_ref[0:ROWS].astype(f32)
    far = far_ref[...].astype(f32)
    source_ref[0:8] = near[0:8] + joints[8:16] * correction(far[0:8])
    source_ref[8:ROWS] = near[8:]
    source_ref[ROWS:] = head_k1 * mine
    medium_part(source_ref, taps_ref, sums_ref, -1, (-16, 0), partial_ref)
    filtered = sums_ref[0, 8 : 8 + ROWS]
    for shift in range(1, 8):
        filtered += sums_ref[shift, 8 - shift : 8 - shift + ROWS]
    stream = jnp.concatenate([mine, stream_ref[...].astype(f32)[8:]], axis=0)
    stream = (stream + field_of(fields, 1, 0) * filtered).astype(bf16)
    next_ref[...] = stream
    stream = stream.astype(f32)
    gated = field_of(fields, 2, 1) * stream
    gated_ref[...] = gated
    powers = [powers_ref[age] for age in range(9)]
    state = jnp.zeros((8, WIDTH), f32)
    before_last = state
    for group in range(16):
        step = powers[7] * gated[8 * group : 8 * group + 1]
        for row in range(1, 8):
            step += powers[7 - row] * gated[8 * group + row : 8 * group + row + 1]
        steps_ref[group] = step
        before_last = state
        state = powers[8] * state + step
    sent = jnp.concatenate([state[:, :128], state[:, 128:]], axis=0).astype(bf16)
    ends_ref[...] = jnp.broadcast_to(sent[None], ends_ref.shape)
    last = gated[ROWS - 8 :]
    pad_ref[8:16] = last
    sums = within_rows(kernel_ref, last, pad_ref) + carried_rows(carry_ref, before_last)
    q2 = field_of(fields, 2, 0, pl.ds(ROWS - 16, 16))[8:]
    k3 = field_of(fields, 3, 1, pl.ds(ROWS - 16, 16))[8:]
    tail_ref[...] = k3 * (stream[ROWS - 8 :] + q2 * sums)


def within_kernel(gated_ref, kernel_ref, local_ref, pad_ref):
    gated = gated_ref[...]
    pad_ref[0:8] = jnp.zeros((8, WIDTH), f32)
    pad_ref[8:] = gated
    local_ref[...] = within_rows(kernel_ref, gated, pad_ref)


def third_kernel(
    local_ref, steps_ref, stream_ref, ends_ref, tail_ref, near_ref, short_ref,
    rates_ref, powers_ref, carry_ref, f0, f1, f2, f3,
    out_ref, sums_ref, pad_ref,
):
    fields = (f0, f1, f2, f3)
    lanes = lanes_of(lax.axis_index("sec"))
    mine = lax.axis_index("ctx")
    rates = rates_ref[:, lanes]
    span = jnp.exp(-rates * ROWS)
    state = jnp.zeros((8, WIDTH), f32)
    previous = state
    for position in range(CTX - 1):
        received = ends_ref[position].astype(f32)
        longer = span * state + jnp.concatenate([received[0:8], received[8:16]], axis=1)
        previous = jnp.where(position < mine - 1, longer, previous)
        state = jnp.where(position < mine, longer, state)
    carried = carried_rows(carry_ref, jnp.exp(-rates * (ROWS - 8)) * previous)
    gates = near_ref[ROWS + 16 :].astype(f32)[8:]
    pad_ref[0:8] = tail_ref[...] + gates * carried
    for group in range(16):
        rows = slice(8 * group, 8 * group + 8)
        sums_ref[rows] = local_ref[rows] + carried_rows(carry_ref, state)
        state = powers_ref[8] * state + steps_ref[group]
    stream = stream_ref[...].astype(f32) + field_of(fields, 2, 0) * sums_ref[...]
    stream = stream.astype(bf16).astype(f32)
    pad_ref[8:] = field_of(fields, 3, 1) * stream
    filtered = short_sum(pad_ref, short_ref[1, :, lanes])
    out_ref[...] = (stream + field_of(fields, 3, 0) * filtered).astype(bf16)


def shape(dims, dtype):
    return jax.ShapeDtypeStruct(dims, dtype)


def call(kernel, outs, scratch, operands, name, in_hbm=(), out_hbm=(), flops=1000000, room=32):
    vmem = pl.BlockSpec(memory_space=pltpu.VMEM)
    return pl.pallas_call(
        kernel,
        out_shape=outs,
        in_specs=[
            pl.BlockSpec(memory_space=pl.ANY) if index in in_hbm else vmem
            for index in range(len(operands))
        ],
        out_specs=[
            pl.BlockSpec(memory_space=pl.ANY) if index in out_hbm else vmem
            for index in range(len(outs))
        ],
        scratch_shapes=scratch,
        compiler_params=pltpu.CompilerParams(vmem_limit_bytes=room * 1024 * 1024),
        cost_estimate=pl.CostEstimate(flops=flops, bytes_accessed=1000000, transcendentals=0),
        name=name,
    )(*operands)


def shards(x, q, k, gain, short, medium, rates, residues, direct):
    gain, direct = gain[None], direct[None]
    pair = shape((2, ROWS, WIDTH), bf16)
    squares, own, *sends = call(
        pack_kernel,
        [shape((PEERS, 128), f32)] + [pair] * 4,
        [
            pltpu.VMEM((ROWS, WIDTH), bf16),
            pltpu.VMEM((PEERS, 128), f32),
            pltpu.SemaphoreType.DMA((10,)),
        ],
        tuple(pltpu.with_memory_space_constraint(value, pltpu.HBM) for value in (x, q, k)),
        "pack",
        in_hbm=(0, 1, 2),
        out_hbm=(0,),
    )
    fields = [own] + [
        shifted(part, "sec", distance, True) for distance, part in zip(DISTANCES[1:], sends)
    ]
    squares = lax.all_to_all(squares, ("sec", "ch"), 0, 0, tiled=True)
    (entry,) = call(
        entry_kernel, [shape((ROWS, WIDTH), bf16)], [], (x, squares, gain, fields[1], own), "entry", in_hbm=(3,), flops=10**10
    )
    head, stream, gated, halo, far = call(
        first_kernel,
        [
            shape((8, WIDTH), f32),
            shape((ROWS, WIDTH), bf16),
            shape((ROWS, WIDTH), f32),
            shape((ROWS + 32, WIDTH), bf16),
            shape((16, WIDTH), bf16),
        ],
        [pltpu.VMEM((ROWS + 8, WIDTH), f32)],
        (entry, short, *fields),
        "first",
    )
    near_in = shifted(halo, "ctx", 1, False)
    far_in = shifted(far, "ctx", 2, False)
    table = shape((8, 8, WIDTH), f32)
    partial, taps, powers, carry, kernel = call(
        own_kernel,
        [
            shape((8, ROWS - 8, WIDTH), f32),
            shape((8, 16, WIDTH), f32),
            shape((9, 8, WIDTH), f32),
            table,
            table,
        ],
        [],
        (gated, medium, rates, residues, direct),
        "own",
    )
    stream, gated, steps, ends, tail = call(
        second_kernel,
        [
            shape((ROWS, WIDTH), bf16),
            shape((ROWS, WIDTH), f32),
            shape((16, 8, WIDTH), f32),
            shape((CTX, 16, 128), bf16),
            shape((8, WIDTH), f32),
        ],
        [
            pltpu.VMEM((ROWS + 8, WIDTH), f32),
            pltpu.VMEM((8, ROWS + 8, WIDTH), f32),
            pltpu.VMEM((16, WIDTH), f32),
        ],
        (near_in, far_in, head, stream, short, partial, taps, powers, carry, kernel, *fields),
        "second",
    )
    tail_in = shifted(tail, "ctx", 1, False)
    ends = lax.all_to_all(ends, "ctx", 0, 0, tiled=True)
    (local,) = call(
        within_kernel,
        [shape((ROWS, WIDTH), f32)],
        [pltpu.VMEM((ROWS + 8, WIDTH), f32)],
        (gated, kernel),
        "within",
        flops=10**9,
    )
    (out,) = call(
        third_kernel,
        [shape((ROWS, WIDTH), bf16)],
        [pltpu.VMEM((ROWS, WIDTH), f32), pltpu.VMEM((ROWS + 8, WIDTH), f32)],
        (local, steps, stream, ends, tail_in, near_in, short, rates, powers, carry, *fields),
        "third",
    )
    return out


def solution(mesh):
    in_specs = (
        P("ctx", ("ch", "sec")),
        P("sec", "ctx", "ch"),
        P("sec", "ctx", "ch"),
        P("ch"),
        P(None, None, "ch"),
        P(None, "ch"),
        P(None, "ch"),
        P(None, "ch"),
        P("ch"),
    )
    out_specs = P("ctx", ("ch", "sec"))
    return jax.shard_map(shards, mesh=mesh, in_specs=in_specs, out_specs=out_specs, check_vma=False)
```

```python
import jax
import jax.numpy as jnp
from jax import lax
from jax.experimental import pallas as pl
from jax.experimental.pallas import tpu as pltpu
from jax.sharding import PartitionSpec as P

D = 4096
EPS = 1e-06
ROWS = 128
WIDTH = 256
SEC = 4
CTX = 16
PEERS = 16
DISTANCES = (0, 2, 1, 3)
f32 = jnp.float32
bf16 = jnp.bfloat16


def shifted(value, axis, steps, wrap):
    count = lax.axis_size(axis)
    pairs = [
        (source, (source + steps) % count)
        for source in range(count)
        if wrap or 0 <= source + steps < count
    ]
    return lax.ppermute(value, axis, pairs)


def lanes_of(position):
    return pl.ds(pl.multiple_of(position * WIDTH, WIDTH), WIDTH)


def pack_kernel(x_hbm, q_hbm, k_hbm, squares_hbm, own_ref, send_1, send_2, send_3, x_ref, squares_ref, sems):
    sec = lax.axis_index("sec")
    first = pltpu.make_async_copy(x_hbm, x_ref, sems.at[8])
    first.start()
    loads = []
    for slot, (distance, ref) in enumerate(zip(DISTANCES, (own_ref, send_1, send_2, send_3))):
        lanes = lanes_of(lax.rem(sec + distance, SEC))
        for which, source in enumerate((q_hbm, k_hbm)):
            loads.append(
                pltpu.make_async_copy(
                    source.at[0, :, lanes], ref.at[which], sems.at[2 * slot + which]
                )
            )
    for load in loads:
        load.start()
    first.wait()
    x = x_ref[...].astype(f32)
    squared = x * x
    folded = squared[:, :128] + squared[:, 128:]
    squares = jnp.sum(folded.T, axis=0, keepdims=True)
    squares_ref[...] = jnp.broadcast_to(squares, squares_ref.shape)
    loads.append(pltpu.make_async_copy(squares_ref, squares_hbm, sems.at[9]))
    loads[-1].start()
    for load in loads:
        load.wait()


def field_of(refs, section, which, rows=None):
    distance = lax.rem(lax.axis_index("sec") - section + SEC, SEC)

    def read(ref):
        part = ref[which] if rows is None else ref[which, rows]
        return part.astype(f32)

    chosen = read(refs[0])
    for index in range(1, SEC):
        chosen = jnp.where(distance == DISTANCES[index], read(refs[index]), chosen)
    return chosen


def short_sum(padded_ref, taps):
    total = taps[0:1] * padded_ref[8 : 8 + ROWS]
    for tap in range(1, 7):
        total += taps[tap : tap + 1] * padded_ref[8 - tap : 8 - tap + ROWS]
    return total


def entry_kernel(x_ref, squares_ref, gain_ref, across_ref, kept_ref, stream_ref):
    lanes = lanes_of(lax.axis_index("sec"))
    sums = jnp.sum(squares_ref[...], axis=0, keepdims=True)
    inverse = lax.rsqrt(jnp.broadcast_to(sums, (128, 128)).T / D + EPS)
    inverse = jnp.concatenate([inverse, inverse], axis=1)
    stream_ref[...] = (x_ref[...].astype(f32) * inverse * gain_ref[:, lanes]).astype(bf16)


def first_kernel(
    entry_ref, taps_ref, f0, f1, f2, f3,
    head_ref, stream_ref, own_ref, halo_ref, far_ref, pad_ref,
):
    fields = (f0, f1, f2, f3)
    lanes = lanes_of(lax.axis_index("sec"))
    stream = entry_ref[...].astype(f32)
    gated = field_of(fields, 0, 1) * stream
    pad_ref[0:8] = jnp.zeros((8, WIDTH), f32)
    pad_ref[8:] = gated
    filtered = short_sum(pad_ref, taps_ref[0, :, lanes])
    q0 = field_of(fields, 0, 0)
    k1 = field_of(fields, 1, 1)
    raw = stream + q0 * filtered
    head_ref[...] = raw[0:8]
    rounded = raw.astype(bf16)
    stream_ref[...] = rounded
    rounded = rounded.astype(f32)
    gated_1 = jnp.concatenate([k1[0:8] * raw[0:8], k1[8:] * rounded[8:]], axis=0)
    own_ref[...] = gated_1
    halo_ref[0:ROWS] = gated_1.astype(bf16)
    last = gated[ROWS - 8 :]
    gates = k1[0:8] * q0[0:8]
    halo_ref[ROWS : ROWS + 16] = jnp.concatenate([last, gates], axis=0).astype(bf16)
    last_rows = pl.ds(ROWS - 16, 16)
    halo_ref[ROWS + 16 :] = (
        field_of(fields, 2, 0, last_rows) * field_of(fields, 3, 1, last_rows)
    ).astype(bf16)
    far_ref[...] = jnp.concatenate([last, last], axis=0).astype(bf16)


def medium_part(source_ref, taps_ref, partial_ref, low, sources, earlier_ref=None):
    first, last = sources

    def step(index, carry):
        shift = lax.rem(index, 8)
        here = pl.ds(pl.multiple_of((index // 8) * 128, 128), 128)
        taps = [jnp.broadcast_to(taps_ref[shift, a : a + 1, here], (8, 128)) for a in range(16)]
        for group in range(low, 16):
            total = None
            if earlier_ref is not None and group >= 1:
                total = earlier_ref[shift, 8 * group - 8 : 8 * group, here]
            for a in range(16):
                origin = group - a
                if origin < first or origin > last:
                    continue
                start = 8 * (origin - first)
                term = taps[a] * source_ref[start : start + 8, here]
                total = term if total is None else total + term
            start = 8 * (group - low)
            partial_ref[shift, start : start + 8, here] = total
        return carry

    lax.fori_loop(0, 16, step, 0, unroll=2)


def own_kernel(
    gated_ref, medium_ref, rates_ref, residues_ref, direct_ref,
    partial_ref, taps_ref, powers_ref, carry_ref, kernel_ref,
):
    lanes = lanes_of(lax.axis_index("sec"))
    medium_taps = medium_ref[:, lanes].reshape(16, 8, WIDTH)
    for shift in range(8):
        taps_ref[shift] = medium_taps[:, shift]
    medium_part(gated_ref.at[pl.ds(8, ROWS - 8)], taps_ref, partial_ref, 1, (1, 15))
    rates = rates_ref[:, lanes]
    weights = residues_ref[:, lanes] * jnp.sqrt(jnp.tanh(rates) * (1.0 + jnp.exp(-2.0 * rates)))
    position = lax.broadcasted_iota(jnp.int32, (8, WIDTH), 0)
    carries = []
    for age in range(9):
        power = jnp.exp(-rates * age)
        powers_ref[age] = power
        if age < 8:
            row = jnp.sum(weights * power, axis=0, keepdims=True)
            if age == 0:
                row += direct_ref[:, lanes]
            kernel_ref[age] = jnp.where(position >= age, row, 0.0)
        if age > 0:
            carries.append(weights * power)
    carries = jnp.stack(carries, axis=0)
    for mode in range(8):
        carry_ref[mode] = carries[:, mode]


def carried_rows(carry_ref, state):
    total = carry_ref[0] * state[0:1]
    for mode in range(1, 8):
        total += carry_ref[mode] * state[mode : mode + 1]
    return total


def within_rows(kernel_ref, rows, padded_ref):
    count = rows.shape[0]
    grouped = (count // 8, 8, WIDTH)
    total = rows.reshape(grouped) * kernel_ref[0][None]
    for age in range(1, 8):
        total += padded_ref[8 - age : 8 - age + count].reshape(grouped) * kernel_ref[age][None]
    return total.reshape(count, WIDTH)


def second_kernel(
    near_ref, far_ref, head_ref, stream_ref, short_ref,
    partial_ref, taps_ref, powers_ref, carry_ref, kernel_ref, f0, f1, f2, f3,
    next_ref, gated_ref, steps_ref, ends_ref, tail_ref,
    source_ref, sums_ref, pad_ref,
):
    fields = (f0, f1, f2, f3)
    lanes = lanes_of(lax.axis_index("sec"))
    taps = short_ref[0, :, lanes]

    def correction(before):
        pad_ref[0:8] = before
        pad_ref[8:16] = jnp.zeros((8, WIDTH), f32)
        total = jnp.zeros((8, WIDTH), f32)
        for tap in range(1, 7):
            total += taps[tap : tap + 1] * pad_ref[8 - tap : 16 - tap]
        return total

    head_q0 = field_of(fields, 0, 0, pl.ds(0, 16))[0:8]
    head_k1 = field_of(fields, 1, 1, pl.ds(0, 16))[0:8]
    joints = near_ref[ROWS : ROWS + 16].astype(f32)
    mine = (head_ref[...] + head_q0 * correction(joints[0:8])).astype(bf16).astype(f32)
    near = near_ref[0:ROWS].astype(f32)
    far = far_ref[...].astype(f32)
    source_ref[0:8] = near[0:8] + joints[8:16] * correction(far[0:8])
    source_ref[8:ROWS] = near[8:]
    source_ref[ROWS:] = head_k1 * mine
    medium_part(source_ref, taps_ref, sums_ref, -1, (-16, 0), partial_ref)
    filtered = sums_ref[0, 8 : 8 + ROWS]
    for shift in range(1, 8):
        filtered += sums_ref[shift, 8 - shift : 8 - shift + ROWS]
    stream = jnp.concatenate([mine, stream_ref[...].astype(f32)[8:]], axis=0)
    stream = (stream + field_of(fields, 1, 0) * filtered).astype(bf16)
    next_ref[...] = stream
    stream = stream.astype(f32)
    gated = field_of(fields, 2, 1) * stream
    gated_ref[...] = gated
    powers = [powers_ref[age] for age in range(9)]
    state = jnp.zeros((8, WIDTH), f32)
    before_last = state
    for group in range(16):
        step = powers[7] * gated[8 * group : 8 * group + 1]
        for row in range(1, 8):
            step += powers[7 - row] * gated[8 * group + row : 8 * group + row + 1]
        steps_ref[group] = step
        before_last = state
        state = powers[8] * state + step
    sent = jnp.concatenate([state[:, :128], state[:, 128:]], axis=0).astype(bf16)
    ends_ref[...] = jnp.broadcast_to(sent[None], ends_ref.shape)
    last = gated[ROWS - 8 :]
    pad_ref[8:16] = last
    sums = within_rows(kernel_ref, last, pad_ref) + carried_rows(carry_ref, before_last)
    q2 = field_of(fields, 2, 0, pl.ds(ROWS - 16, 16))[8:]
    k3 = field_of(fields, 3, 1, pl.ds(ROWS - 16, 16))[8:]
    tail_ref[...] = k3 * (stream[ROWS - 8 :] + q2 * sums)


def within_kernel(gated_ref, kernel_ref, local_ref, pad_ref):
    gated = gated_ref[...]
    pad_ref[0:8] = jnp.zeros((8, WIDTH), f32)
    pad_ref[8:] = gated
    local_ref[...] = within_rows(kernel_ref, gated, pad_ref)


def third_kernel(
    local_ref, steps_ref, stream_ref, ends_ref, tail_ref, near_ref, short_ref,
    rates_ref, powers_ref, carry_ref, f0, f1, f2, f3,
    out_ref, sums_ref, pad_ref,
):
    fields = (f0, f1, f2, f3)
    lanes = lanes_of(lax.axis_index("sec"))
    mine = lax.axis_index("ctx")
    rates = rates_ref[:, lanes]
    span = jnp.exp(-rates * ROWS)
    state = 0.0 * span
    previous = state

    def join(position, states):
        state, previous = states
        received = ends_ref[position].astype(f32)
        return span * state + jnp.concatenate([received[0:8], received[8:16]], axis=1), state

    state, previous = lax.fori_loop(0, mine, join, (state, previous))
    carried = carried_rows(carry_ref, jnp.exp(-rates * (ROWS - 8)) * previous)
    gates = near_ref[ROWS + 16 :].astype(f32)[8:]
    pad_ref[0:8] = tail_ref[...] + gates * carried
    for group in range(16):
        rows = slice(8 * group, 8 * group + 8)
        sums_ref[rows] = local_ref[rows] + carried_rows(carry_ref, state)
        state = powers_ref[8] * state + steps_ref[group]
    stream = stream_ref[...].astype(f32) + field_of(fields, 2, 0) * sums_ref[...]
    stream = stream.astype(bf16).astype(f32)
    pad_ref[8:] = field_of(fields, 3, 1) * stream
    filtered = short_sum(pad_ref, short_ref[1, :, lanes])
    out_ref[...] = (stream + field_of(fields, 3, 0) * filtered).astype(bf16)


def shape(dims, dtype):
    return jax.ShapeDtypeStruct(dims, dtype)


def call(kernel, outs, scratch, operands, name, in_hbm=(), out_hbm=(), flops=1000000, room=32):
    vmem = pl.BlockSpec(memory_space=pltpu.VMEM)
    return pl.pallas_call(
        kernel,
        out_shape=outs,
        in_specs=[
            pl.BlockSpec(memory_space=pl.ANY) if index in in_hbm else vmem
            for index in range(len(operands))
        ],
        out_specs=[
            pl.BlockSpec(memory_space=pl.ANY) if index in out_hbm else vmem
            for index in range(len(outs))
        ],
        scratch_shapes=scratch,
        compiler_params=pltpu.CompilerParams(vmem_limit_bytes=room * 1024 * 1024),
        cost_estimate=pl.CostEstimate(flops=flops, bytes_accessed=1000000, transcendentals=0),
        name=name,
    )(*operands)


def shards(x, q, k, gain, short, medium, rates, residues, direct):
    gain, direct = gain[None], direct[None]
    pair = shape((2, ROWS, WIDTH), bf16)
    squares, own, *sends = call(
        pack_kernel,
        [shape((PEERS, 128), f32)] + [pair] * 4,
        [
            pltpu.VMEM((ROWS, WIDTH), bf16),
            pltpu.VMEM((PEERS, 128), f32),
            pltpu.SemaphoreType.DMA((10,)),
        ],
        tuple(pltpu.with_memory_space_constraint(value, pltpu.HBM) for value in (x, q, k)),
        "pack",
        in_hbm=(0, 1, 2),
        out_hbm=(0,),
    )
    fields = [own] + [
        shifted(part, "sec", distance, True) for distance, part in zip(DISTANCES[1:], sends)
    ]
    squares = lax.all_to_all(squares, ("sec", "ch"), 0, 0, tiled=True)
    (entry,) = call(
        entry_kernel, [shape((ROWS, WIDTH), bf16)], [], (x, squares, gain, fields[1], own), "entry", in_hbm=(3,), flops=10**10
    )
    head, stream, gated, halo, far = call(
        first_kernel,
        [
            shape((8, WIDTH), f32),
            shape((ROWS, WIDTH), bf16),
            shape((ROWS, WIDTH), f32),
            shape((ROWS + 32, WIDTH), bf16),
            shape((16, WIDTH), bf16),
        ],
        [pltpu.VMEM((ROWS + 8, WIDTH), f32)],
        (entry, short, *fields),
        "first",
    )
    near_in = shifted(halo, "ctx", 1, False)
    far_in = shifted(far, "ctx", 2, False)
    table = shape((8, 8, WIDTH), f32)
    partial, taps, powers, carry, kernel = call(
        own_kernel,
        [
            shape((8, ROWS - 8, WIDTH), f32),
            shape((8, 16, WIDTH), f32),
            shape((9, 8, WIDTH), f32),
            table,
            table,
        ],
        [],
        (gated, medium, rates, residues, direct),
        "own",
    )
    stream, gated, steps, ends, tail = call(
        second_kernel,
        [
            shape((ROWS, WIDTH), bf16),
            shape((ROWS, WIDTH), f32),
            shape((16, 8, WIDTH), f32),
            shape((CTX, 16, 128), bf16),
            shape((8, WIDTH), f32),
        ],
        [
            pltpu.VMEM((ROWS + 8, WIDTH), f32),
            pltpu.VMEM((8, ROWS + 8, WIDTH), f32),
            pltpu.VMEM((16, WIDTH), f32),
        ],
        (near_in, far_in, head, stream, short, partial, taps, powers, carry, kernel, *fields),
        "second",
    )
    tail_in = shifted(tail, "ctx", 1, False)
    ends = lax.all_to_all(ends, "ctx", 0, 0, tiled=True)
    (local,) = call(
        within_kernel,
        [shape((ROWS, WIDTH), f32)],
        [pltpu.VMEM((ROWS + 8, WIDTH), f32)],
        (gated, kernel),
        "within",
        flops=10**9,
    )
    (out,) = call(
        third_kernel,
        [shape((ROWS, WIDTH), bf16)],
        [pltpu.VMEM((ROWS, WIDTH), f32), pltpu.VMEM((ROWS + 8, WIDTH), f32)],
        (local, steps, stream, ends, tail_in, near_in, short, rates, powers, carry, *fields),
        "third",
    )
    return out


def solution(mesh):
    in_specs = (
        P("ctx", ("ch", "sec")),
        P("sec", "ctx", "ch"),
        P("sec", "ctx", "ch"),
        P("ch"),
        P(None, None, "ch"),
        P(None, "ch"),
        P(None, "ch"),
        P(None, "ch"),
        P("ch"),
    )
    out_specs = P("ctx", ("ch", "sec"))
    return jax.shard_map(shards, mesh=mesh, in_specs=in_specs, out_specs=out_specs, check_vma=False)
```

```python
import jax
import jax.numpy as jnp
from jax import lax
from jax.experimental import pallas as pl
from jax.experimental.pallas import tpu as pltpu
from jax.sharding import PartitionSpec as P

D = 4096
EPS = 1e-06
ROWS = 128
WIDTH = 256
SEC = 4
CTX = 16
PEERS = 16
DISTANCES = (0, 2, 1, 3)
f32 = jnp.float32
bf16 = jnp.bfloat16


def shifted(value, axis, steps, wrap):
    count = lax.axis_size(axis)
    pairs = [
        (source, (source + steps) % count)
        for source in range(count)
        if wrap or 0 <= source + steps < count
    ]
    return lax.ppermute(value, axis, pairs)


def lanes_of(position):
    return pl.ds(pl.multiple_of(position * WIDTH, WIDTH), WIDTH)


def pack_kernel(x_hbm, q_hbm, k_hbm, squares_hbm, own_ref, send_1, send_2, send_3, x_ref, squares_ref, sems):
    sec = lax.axis_index("sec")
    first = pltpu.make_async_copy(x_hbm, x_ref, sems.at[8])
    first.start()
    loads = []
    for slot, (distance, ref) in enumerate(zip(DISTANCES, (own_ref, send_1, send_2, send_3))):
        lanes = lanes_of(lax.rem(sec + distance, SEC))
        for which, source in enumerate((q_hbm, k_hbm)):
            loads.append(
                pltpu.make_async_copy(
                    source.at[0, :, lanes], ref.at[which], sems.at[2 * slot + which]
                )
            )
    for load in loads:
        load.start()
    first.wait()
    x = x_ref[...].astype(f32)
    squared = x * x
    folded = squared[:, :128] + squared[:, 128:]
    squares = jnp.sum(folded.T, axis=0, keepdims=True)
    squares_ref[...] = jnp.broadcast_to(squares, squares_ref.shape)
    loads.append(pltpu.make_async_copy(squares_ref, squares_hbm, sems.at[9]))
    loads[-1].start()
    for load in loads:
        load.wait()


def field_of(refs, section, which, rows=None):
    distance = lax.rem(lax.axis_index("sec") - section + SEC, SEC)

    def read(ref):
        part = ref[which] if rows is None else ref[which, rows]
        return part.astype(f32)

    chosen = read(refs[0])
    for index in range(1, SEC):
        chosen = jnp.where(distance == DISTANCES[index], read(refs[index]), chosen)
    return chosen


def short_sum(padded_ref, taps):
    total = taps[0:1] * padded_ref[8 : 8 + ROWS]
    for tap in range(1, 7):
        total += taps[tap : tap + 1] * padded_ref[8 - tap : 8 - tap + ROWS]
    return total


def entry_kernel(x_ref, squares_ref, gain_ref, across_ref, kept_ref, stream_ref):
    lanes = lanes_of(lax.axis_index("sec"))
    sums = jnp.sum(squares_ref[...], axis=0, keepdims=True)
    inverse = lax.rsqrt(jnp.broadcast_to(sums, (128, 128)).T / D + EPS)
    inverse = jnp.concatenate([inverse, inverse], axis=1)
    stream_ref[...] = (x_ref[...].astype(f32) * inverse * gain_ref[:, lanes]).astype(bf16)


def first_kernel(
    entry_ref, taps_ref, f0, f1, f2, f3,
    head_ref, stream_ref, own_ref, halo_ref, far_ref, pad_ref,
):
    fields = (f0, f1, f2, f3)
    lanes = lanes_of(lax.axis_index("sec"))
    stream = entry_ref[...].astype(f32)
    gated = field_of(fields, 0, 1) * stream
    pad_ref[0:8] = jnp.zeros((8, WIDTH), f32)
    pad_ref[8:] = gated
    filtered = short_sum(pad_ref, taps_ref[0, :, lanes])
    q0 = field_of(fields, 0, 0)
    k1 = field_of(fields, 1, 1)
    raw = stream + q0 * filtered
    head_ref[...] = raw[0:8]
    rounded = raw.astype(bf16)
    stream_ref[...] = rounded
    rounded = rounded.astype(f32)
    gated_1 = jnp.concatenate([k1[0:8] * raw[0:8], k1[8:] * rounded[8:]], axis=0)
    own_ref[...] = gated_1
    halo_ref[0:ROWS] = gated_1.astype(bf16)
    last = gated[ROWS - 8 :]
    gates = k1[0:8] * q0[0:8]
    halo_ref[ROWS : ROWS + 16] = jnp.concatenate([last, gates], axis=0).astype(bf16)
    last_rows = pl.ds(ROWS - 16, 16)
    halo_ref[ROWS + 16 :] = (
        field_of(fields, 2, 0, last_rows) * field_of(fields, 3, 1, last_rows)
    ).astype(bf16)
    far_ref[...] = jnp.concatenate([last, last], axis=0).astype(bf16)


def medium_part(source_ref, taps_ref, partial_ref, low, sources, earlier_ref=None):
    first, last = sources

    def step(index, carry):
        shift = lax.rem(index, 8)
        here = pl.ds(pl.multiple_of((index // 8) * 128, 128), 128)
        taps = [jnp.broadcast_to(taps_ref[shift, a : a + 1, here], (8, 128)) for a in range(16)]
        for group in range(low, 16):
            total = None
            if earlier_ref is not None and group >= 1:
                total = earlier_ref[shift, 8 * group - 8 : 8 * group, here]
            for a in range(16):
                origin = group - a
                if origin < first or origin > last:
                    continue
                start = 8 * (origin - first)
                term = taps[a] * source_ref[start : start + 8, here]
                total = term if total is None else total + term
            start = 8 * (group - low)
            partial_ref[shift, start : start + 8, here] = total
        return carry

    lax.fori_loop(0, 16, step, 0, unroll=4)


def own_kernel(
    gated_ref, medium_ref, rates_ref, residues_ref, direct_ref,
    partial_ref, taps_ref, powers_ref, carry_ref, kernel_ref,
):
    lanes = lanes_of(lax.axis_index("sec"))
    medium_taps = medium_ref[:, lanes].reshape(16, 8, WIDTH)
    for shift in range(8):
        taps_ref[shift] = medium_taps[:, shift]
    medium_part(gated_ref.at[pl.ds(8, ROWS - 8)], taps_ref, partial_ref, 1, (1, 15))
    rates = rates_ref[:, lanes]
    weights = residues_ref[:, lanes] * jnp.sqrt(jnp.tanh(rates) * (1.0 + jnp.exp(-2.0 * rates)))
    position = lax.broadcasted_iota(jnp.int32, (8, WIDTH), 0)
    carries = []
    for age in range(9):
        power = jnp.exp(-rates * age)
        powers_ref[age] = power
        if age < 8:
            row = jnp.sum(weights * power, axis=0, keepdims=True)
            if age == 0:
                row += direct_ref[:, lanes]
            kernel_ref[age] = jnp.where(position >= age, row, 0.0)
        if age > 0:
            carries.append(weights * power)
    carries = jnp.stack(carries, axis=0)
    for mode in range(8):
        carry_ref[mode] = carries[:, mode]


def carried_rows(carry_ref, state):
    total = carry_ref[0] * state[0:1]
    for mode in range(1, 8):
        total += carry_ref[mode] * state[mode : mode + 1]
    return total


def within_rows(kernel_ref, rows, padded_ref):
    count = rows.shape[0]
    grouped = (count // 8, 8, WIDTH)
    total = rows.reshape(grouped) * kernel_ref[0][None]
    for age in range(1, 8):
        total += padded_ref[8 - age : 8 - age + count].reshape(grouped) * kernel_ref[age][None]
    return total.reshape(count, WIDTH)


def second_kernel(
    near_ref, far_ref, head_ref, stream_ref, short_ref,
    partial_ref, taps_ref, powers_ref, carry_ref, kernel_ref, f0, f1, f2, f3,
    next_ref, gated_ref, steps_ref, ends_ref, tail_ref,
    source_ref, sums_ref, pad_ref,
):
    fields = (f0, f1, f2, f3)
    lanes = lanes_of(lax.axis_index("sec"))
    taps = short_ref[0, :, lanes]

    def correction(before):
        pad_ref[0:8] = before
        pad_ref[8:16] = jnp.zeros((8, WIDTH), f32)
        total = jnp.zeros((8, WIDTH), f32)
        for tap in range(1, 7):
            total += taps[tap : tap + 1] * pad_ref[8 - tap : 16 - tap]
        return total

    head_q0 = field_of(fields, 0, 0, pl.ds(0, 16))[0:8]
    head_k1 = field_of(fields, 1, 1, pl.ds(0, 16))[0:8]
    joints = near_ref[ROWS : ROWS + 16].astype(f32)
    mine = (head_ref[...] + head_q0 * correction(joints[0:8])).astype(bf16).astype(f32)
    near = near_ref[0:ROWS].astype(f32)
    far = far_ref[...].astype(f32)
    source_ref[0:8] = near[0:8] + joints[8:16] * correction(far[0:8])
    source_ref[8:ROWS] = near[8:]
    source_ref[ROWS:] = head_k1 * mine
    medium_part(source_ref, taps_ref, sums_ref, -1, (-16, 0), partial_ref)
    filtered = sums_ref[0, 8 : 8 + ROWS]
    for shift in range(1, 8):
        filtered += sums_ref[shift, 8 - shift : 8 - shift + ROWS]
    stream = jnp.concatenate([mine, stream_ref[...].astype(f32)[8:]], axis=0)
    stream = (stream + field_of(fields, 1, 0) * filtered).astype(bf16)
    next_ref[...] = stream
    stream = stream.astype(f32)
    gated = field_of(fields, 2, 1) * stream
    gated_ref[...] = gated
    powers = [powers_ref[age] for age in range(9)]
    state = jnp.zeros((8, WIDTH), f32)
    before_last = state
    for group in range(16):
        step = powers[7] * gated[8 * group : 8 * group + 1]
        for row in range(1, 8):
            step += powers[7 - row] * gated[8 * group + row : 8 * group + row + 1]
        steps_ref[group] = step
        before_last = state
        state = powers[8] * state + step
    sent = jnp.concatenate([state[:, :128], state[:, 128:]], axis=0).astype(bf16)
    ends_ref[...] = jnp.broadcast_to(sent[None], ends_ref.shape)
    last = gated[ROWS - 8 :]
    pad_ref[8:16] = last
    sums = within_rows(kernel_ref, last, pad_ref) + carried_rows(carry_ref, before_last)
    q2 = field_of(fields, 2, 0, pl.ds(ROWS - 16, 16))[8:]
    k3 = field_of(fields, 3, 1, pl.ds(ROWS - 16, 16))[8:]
    tail_ref[...] = k3 * (stream[ROWS - 8 :] + q2 * sums)


def within_kernel(gated_ref, kernel_ref, local_ref, pad_ref):
    gated = gated_ref[...]
    pad_ref[0:8] = jnp.zeros((8, WIDTH), f32)
    pad_ref[8:] = gated
    local_ref[...] = within_rows(kernel_ref, gated, pad_ref)


def third_kernel(
    local_ref, steps_ref, stream_ref, ends_ref, tail_ref, near_ref, short_ref,
    rates_ref, powers_ref, carry_ref, f0, f1, f2, f3,
    out_ref, sums_ref, pad_ref,
):
    fields = (f0, f1, f2, f3)
    lanes = lanes_of(lax.axis_index("sec"))
    mine = lax.axis_index("ctx")
    rates = rates_ref[:, lanes]
    span = jnp.exp(-rates * ROWS)
    state = jnp.zeros((8, WIDTH), f32)
    previous = state
    for position in range(CTX - 1):
        received = ends_ref[position].astype(f32)
        longer = span * state + jnp.concatenate([received[0:8], received[8:16]], axis=1)
        previous = jnp.where(position < mine - 1, longer, previous)
        state = jnp.where(position < mine, longer, state)
    carried = carried_rows(carry_ref, jnp.exp(-rates * (ROWS - 8)) * previous)
    gates = near_ref[ROWS + 16 :].astype(f32)[8:]
    pad_ref[0:8] = tail_ref[...] + gates * carried
    for group in range(16):
        rows = slice(8 * group, 8 * group + 8)
        sums_ref[rows] = local_ref[rows] + carried_rows(carry_ref, state)
        state = powers_ref[8] * state + steps_ref[group]
    stream = stream_ref[...].astype(f32) + field_of(fields, 2, 0) * sums_ref[...]
    stream = stream.astype(bf16).astype(f32)
    pad_ref[8:] = field_of(fields, 3, 1) * stream
    filtered = short_sum(pad_ref, short_ref[1, :, lanes])
    out_ref[...] = (stream + field_of(fields, 3, 0) * filtered).astype(bf16)


def shape(dims, dtype):
    return jax.ShapeDtypeStruct(dims, dtype)


def call(kernel, outs, scratch, operands, name, in_hbm=(), out_hbm=(), flops=1000000, room=32):
    vmem = pl.BlockSpec(memory_space=pltpu.VMEM)
    return pl.pallas_call(
        kernel,
        out_shape=outs,
        in_specs=[
            pl.BlockSpec(memory_space=pl.ANY) if index in in_hbm else vmem
            for index in range(len(operands))
        ],
        out_specs=[
            pl.BlockSpec(memory_space=pl.ANY) if index in out_hbm else vmem
            for index in range(len(outs))
        ],
        scratch_shapes=scratch,
        compiler_params=pltpu.CompilerParams(vmem_limit_bytes=room * 1024 * 1024),
        cost_estimate=pl.CostEstimate(flops=flops, bytes_accessed=1000000, transcendentals=0),
        name=name,
    )(*operands)


def shards(x, q, k, gain, short, medium, rates, residues, direct):
    gain, direct = gain[None], direct[None]
    pair = shape((2, ROWS, WIDTH), bf16)
    squares, own, *sends = call(
        pack_kernel,
        [shape((PEERS, 128), f32)] + [pair] * 4,
        [
            pltpu.VMEM((ROWS, WIDTH), bf16),
            pltpu.VMEM((PEERS, 128), f32),
            pltpu.SemaphoreType.DMA((10,)),
        ],
        tuple(pltpu.with_memory_space_constraint(value, pltpu.HBM) for value in (x, q, k)),
        "pack",
        in_hbm=(0, 1, 2),
        out_hbm=(0,),
    )
    fields = [own] + [
        shifted(part, "sec", distance, True) for distance, part in zip(DISTANCES[1:], sends)
    ]
    squares = lax.all_to_all(squares, ("sec", "ch"), 0, 0, tiled=True)
    (entry,) = call(
        entry_kernel, [shape((ROWS, WIDTH), bf16)], [], (x, squares, gain, fields[1], own), "entry", in_hbm=(3,), flops=10**10
    )
    head, stream, gated, halo, far = call(
        first_kernel,
        [
            shape((8, WIDTH), f32),
            shape((ROWS, WIDTH), bf16),
            shape((ROWS, WIDTH), f32),
            shape((ROWS + 32, WIDTH), bf16),
            shape((16, WIDTH), bf16),
        ],
        [pltpu.VMEM((ROWS + 8, WIDTH), f32)],
        (entry, short, *fields),
        "first",
    )
    near_in = shifted(halo, "ctx", 1, False)
    far_in = shifted(far, "ctx", 2, False)
    table = shape((8, 8, WIDTH), f32)
    partial, taps, powers, carry, kernel = call(
        own_kernel,
        [
            shape((8, ROWS - 8, WIDTH), f32),
            shape((8, 16, WIDTH), f32),
            shape((9, 8, WIDTH), f32),
            table,
            table,
        ],
        [],
        (gated, medium, rates, residues, direct),
        "own",
    )
    stream, gated, steps, ends, tail = call(
        second_kernel,
        [
            shape((ROWS, WIDTH), bf16),
            shape((ROWS, WIDTH), f32),
            shape((16, 8, WIDTH), f32),
            shape((CTX, 16, 128), bf16),
            shape((8, WIDTH), f32),
        ],
        [
            pltpu.VMEM((ROWS + 8, WIDTH), f32),
            pltpu.VMEM((8, ROWS + 8, WIDTH), f32),
            pltpu.VMEM((16, WIDTH), f32),
        ],
        (near_in, far_in, head, stream, short, partial, taps, powers, carry, kernel, *fields),
        "second",
    )
    tail_in = shifted(tail, "ctx", 1, False)
    ends = lax.all_to_all(ends, "ctx", 0, 0, tiled=True)
    (local,) = call(
        within_kernel,
        [shape((ROWS, WIDTH), f32)],
        [pltpu.VMEM((ROWS + 8, WIDTH), f32)],
        (gated, kernel),
        "within",
        flops=10**9,
    )
    (out,) = call(
        third_kernel,
        [shape((ROWS, WIDTH), bf16)],
        [pltpu.VMEM((ROWS, WIDTH), f32), pltpu.VMEM((ROWS + 8, WIDTH), f32)],
        (local, steps, stream, ends, tail_in, near_in, short, rates, powers, carry, *fields),
        "third",
    )
    return out


def solution(mesh):
    in_specs = (
        P("ctx", ("ch", "sec")),
        P("sec", "ctx", "ch"),
        P("sec", "ctx", "ch"),
        P("ch"),
        P(None, None, "ch"),
        P(None, "ch"),
        P(None, "ch"),
        P(None, "ch"),
        P("ch"),
    )
    out_specs = P("ctx", ("ch", "sec"))
    return jax.shard_map(shards, mesh=mesh, in_specs=in_specs, out_specs=out_specs, check_vma=False)
```
